256 devices in a mesh: dp: 4 (over y_hi, core), seq: 64 (over z, y_lo, x).
Axes of the slice: x: 4, y: 4 (y_hi: 2, y_lo: 2; y = y_hi * 2 + y_lo), z: 8, core: 2. Of those that a mesh axis runs over, the one named last changes fastest.
Arguments:
- space_query: bfloat16 [256, 704, 576], P(('dp', 'seq')), parts along dimension 0, may hold values from -8 to 8
- space_key: bfloat16 [256, 704, 576], P(('dp', 'seq')), parts along dimension 0, may hold values from -8 to 8
- space_value: bfloat16 [256, 704, 576], P(('dp', 'seq')), parts along dimension 0, may hold values from -6 to 6
- space_output: bfloat16 [256, 704, 576], P(('dp', 'seq')), parts along dimension 0, may hold values from -6 to 6
- space_upstream: bfloat16 [256, 704, 576], P(('dp', 'seq')), parts along dimension 0, may hold values from -6 to 6
- time_query: bfloat16 [256, 704, 576], P(('dp', 'seq')), parts along dimension 0, may hold values from -8 to 8
- time_key: bfloat16 [256, 704, 576], P(('dp', 'seq')), parts along dimension 0, may hold values from -8 to 8
- time_value: bfloat16 [256, 704, 576], P(('dp', 'seq')), parts along dimension 0, may hold values from -6 to 6
- time_output: bfloat16 [256, 704, 576], P(('dp', 'seq')), parts along dimension 0, may hold values from -6 to 6
- time_upstream: bfloat16 [256, 704, 576], P(('dp', 'seq')), parts along dimension 0, may hold values from -6 to 6
Outputs:
- space_query_grad: bfloat16 [256, 704, 576], P(('dp', 'seq')), parts along dimension 0
- space_key_grad: bfloat16 [256, 704, 576], P(('dp', 'seq')), parts along dimension 0
- space_value_grad: bfloat16 [256, 704, 576], P(('dp', 'seq')), parts along dimension 0
- time_query_grad: bfloat16 [256, 704, 576], P(('dp', 'seq')), parts along dimension 0
- time_key_grad: bfloat16 [256, 704, 576], P(('dp', 'seq')), parts along dimension 0
- time_value_grad: bfloat16 [256, 704, 576], P(('dp', 'seq')), parts along dimension 0
The draws below stay inside these ranges and needn't reach their ends.
There are 4 independent parts, one for each index of `dp`. The reference program is written for one: setup_inputs(seed, part) draws one part's arguments, and reference() takes and returns one part's arrays. A program takes and returns all parts, laid end to end along the dimension named above; each array names one. Nothing has to cross between parts.
All inputs are finite; a program needn't handle non-finite values.
Results may differ from the reference program's by a relative error of at most 0.0054.
Values may be sent and summed in bfloat16 or wider, within the bound.
No kernel may reach another device: no remote copies, remote signals or barrier semaphores. Data moves between devices by JAX's collectives and lax.ppermute only.
A program may use at most 64 MiB of HBM per device.

```python
import math
import jax
import jax.numpy as jnp
from jax import lax

FRAME_TOK = 704
HEADS = 8
HEAD_DIM = 72
FRAMES = 64


def pair_parts(key):
    shape = (FRAMES, FRAME_TOK, HEADS, HEAD_DIM)
    split_keys = jax.random.split(key, 6)
    drawn_q = jax.random.normal(split_keys[0], shape, jnp.float32)
    drawn_k = jax.random.normal(split_keys[1], shape, jnp.float32)
    scale_shape = (FRAMES, FRAME_TOK, HEADS, 1)
    scale_q = jnp.exp(jax.random.uniform(split_keys[4], scale_shape, jnp.float32, minval=math.log(0.3), maxval=math.log(3.0)))
    scale_k = jnp.exp(jax.random.uniform(split_keys[5], scale_shape, jnp.float32, minval=math.log(0.3), maxval=math.log(3.0)))
    return (drawn_q, drawn_k, scale_q, scale_k)


def finish(values):
    return jnp.clip(values, -8.0, 8.0).reshape(FRAMES, FRAME_TOK, HEADS * HEAD_DIM).astype(jnp.bfloat16)


def draw_space_query(key, part):
    key = jax.random.fold_in(key, 11)
    drawn_q, drawn_k, scale_q, scale_k = pair_parts(key)
    queries = drawn_q * scale_q
    return finish(queries)


def draw_space_key(key, part):
    key = jax.random.fold_in(key, 11)
    drawn_q, drawn_k, scale_q, scale_k = pair_parts(key)
    key_rows = drawn_k * scale_k
    return finish(key_rows)


def draw_time_query(key, part):
    key = jax.random.fold_in(key, 12)
    drawn_q, drawn_k, scale_q, scale_k = pair_parts(key)
    queries = drawn_q * scale_q
    return finish(queries)


def draw_time_key(key, part):
    key = jax.random.fold_in(key, 12)
    drawn_q, drawn_k, scale_q, scale_k = pair_parts(key)
    key_rows = drawn_k * scale_k
    return finish(key_rows)


def levels(own_key, dims, cuts, low, largest):
    factor_of, own = 1.0, jax.random.fold_in(own_key, 6)
    for axis_at, blocks in cuts:
        draws = jnp.exp(jax.random.uniform(jax.random.fold_in(own, axis_at), (blocks,), jnp.float32, low / len(cuts), largest / len(cuts)))
        factor_of = factor_of * jnp.repeat(draws, dims[axis_at] // blocks).reshape([-1 if axis == axis_at else 1 for axis in range(len(dims))])
    return factor_of


def gaussian(key, dims, deviation, most, cuts=(), held_as=jnp.bfloat16):
    array = deviation * jax.random.normal(key, dims, jnp.float32)
    if cuts:
        array = array * levels(key, dims, cuts, -0.22, 0.18)
    return jnp.clip(array, -most, most).astype(held_as)


def setup_inputs(seed: int = 0, part: int = 0) -> dict:
    seeds = jax.random.split(jax.random.key(seed), 11)
    part_keys = jax.random.split(jax.random.fold_in(seeds[10], part), 11)
    return {
        "space_query": draw_space_query(jax.random.fold_in(jax.random.fold_in(seeds[10], part), 71), part),
        "space_key": draw_space_key(jax.random.fold_in(jax.random.fold_in(seeds[10], part), 71), part),
        "space_value": gaussian(part_keys[2], (FRAMES, FRAME_TOK, HEADS * HEAD_DIM), 1.0, 6.0, ((0, 64),)),
        "space_output": gaussian(part_keys[3], (FRAMES, FRAME_TOK, HEADS * HEAD_DIM), 1.0, 6.0, ((0, 64),)),
        "space_upstream": gaussian(part_keys[4], (FRAMES, FRAME_TOK, HEADS * HEAD_DIM), 1.0, 6.0, ((0, 64),)),
        "time_query": draw_time_query(jax.random.fold_in(jax.random.fold_in(seeds[10], part), 71), part),
        "time_key": draw_time_key(jax.random.fold_in(jax.random.fold_in(seeds[10], part), 71), part),
        "time_value": gaussian(part_keys[7], (FRAMES, FRAME_TOK, HEADS * HEAD_DIM), 1.0, 6.0, ((0, 64),)),
        "time_output": gaussian(part_keys[8], (FRAMES, FRAME_TOK, HEADS * HEAD_DIM), 1.0, 6.0, ((0, 64),)),
        "time_upstream": gaussian(part_keys[9], (FRAMES, FRAME_TOK, HEADS * HEAD_DIM), 1.0, 6.0, ((0, 64),)),
    }


def softmax_grads(queries, key_rows, values, upstream, row_dot, layout):
    mirror = layout.replace('l', 'm')
    scaling = 1.0 / math.sqrt(queries.shape[-1])
    scores = jnp.einsum(layout + ',' + mirror + '->bhlm', queries, key_rows) * scaling
    row_max = lax.optimization_barrier(jnp.max(scores, axis=-1, keepdims=True))
    weights = jnp.exp(scores - row_max)
    attend = weights / lax.optimization_barrier(jnp.sum(weights, axis=-1, keepdims=True))
    attend_low = lax.optimization_barrier(attend.astype(jnp.bfloat16)).astype(jnp.float32)
    grad_values = jnp.einsum('bhlm,' + layout + '->' + mirror, attend_low, upstream)
    grad_attend = jnp.einsum(layout + ',' + mirror + '->bhlm', upstream, values)
    shifted = grad_attend - jnp.einsum(layout.replace('e', '') + '->bhl', row_dot)[..., None]
    dscore = lax.optimization_barrier((attend * shifted).astype(jnp.bfloat16)).astype(jnp.float32)
    grad_queries = jnp.einsum('bhlm,' + mirror + '->' + layout, dscore, key_rows) * scaling
    grad_keys = jnp.einsum('bhlm,' + layout + '->' + mirror, dscore, queries) * scaling
    return (grad_queries.astype(jnp.bfloat16), grad_keys.astype(jnp.bfloat16), grad_values.astype(jnp.bfloat16))

def reference(space_query, space_key, space_value, space_output, space_upstream, time_query, time_key, time_value, time_output, time_upstream):
    width = HEADS * HEAD_DIM

    def frame_grads(pieces):
        parted = [member.reshape(1, FRAME_TOK, HEADS, HEAD_DIM).astype(jnp.float32) for member in pieces]
        row_dot = lax.optimization_barrier(jnp.sum(parted[4] * parted[3], axis=-1))
        grads = softmax_grads(parted[0], parted[1], parted[2], parted[4], row_dot, 'blhe')
        return tuple((member.reshape(FRAME_TOK, width) for member in grads))
    space_grads = lax.map(frame_grads, (space_query, space_key, space_value, space_output, space_upstream))
    parted = [member.reshape(FRAMES, FRAME_TOK, HEADS, HEAD_DIM).astype(jnp.float32) for member in (time_query, time_key, time_value, time_output, time_upstream)]
    time_dot = lax.optimization_barrier(jnp.sum(parted[4] * parted[3], axis=-1))
    time_dot = lax.optimization_barrier(time_dot.astype(jnp.bfloat16)).astype(jnp.float32)
    time_grads = softmax_grads(parted[0], parted[1], parted[2], parted[4], time_dot, 'lbhe')
    time_grads = [member.reshape(FRAMES, FRAME_TOK, width) for member in time_grads]
    return (space_grads[0], space_grads[1], space_grads[2], time_grads[0], time_grads[1], time_grads[2])
```

```python
import functools
import math

import jax
import jax.numpy as jnp
from jax import lax
from jax.experimental import pallas as pl
from jax.experimental.pallas import tpu as pltpu
from jax.sharding import PartitionSpec as P

HEADS = 8
DIM = 72
WIDTH = HEADS * DIM
TOKENS = 704
FRAMES = 64
BULK = 8 * FRAMES
EXTRA = TOKENS - BULK
GROUPS = EXTRA // 64
SEND = 3200
BACK = 2432
DOT_LANE = 96
SCALE = 1.0 / math.sqrt(DIM)
EXP_SCALE = SCALE * math.log2(math.e)
VMEM = 50 * 1024 * 1024
BF16 = jnp.bfloat16
F32 = jnp.float32


def dot(a, b, dims):
    return lax.dot_general(a, b, (dims, ((), ())), preferred_element_type=F32)


def split(x):
    high = x.astype(BF16)
    return high, (x - high.astype(F32)).astype(BF16)


def deal(rows, head):
    cut = rows[:, head * DIM : (head + 1) * DIM].reshape(8, GROUPS, 8, DIM)
    return [cut[:, j] for j in range(GROUPS)]


def pack_kernel(q_ref, k_ref, v_ref, g_ref, o_ref, out_ref):
    members = (q_ref, k_ref, v_ref, g_ref)
    for c, ref in enumerate(members):
        out_ref[:, c * WIDTH : (c + 1) * WIDTH] = ref[0:BULK, :]
    prod = g_ref[0:BULK, :].astype(F32) * o_ref[0:BULK, :].astype(F32)
    high, low = split(prod)
    column = lax.broadcasted_iota(jnp.int32, (WIDTH, 128), 0)
    lane = lax.broadcasted_iota(jnp.int32, (WIDTH, 128), 1) - DOT_LANE
    inside = (column >= lane * DIM) & (column < (lane + 1) * DIM) & (lane >= 0)
    pick = jnp.where(inside, 1.0, 0.0).astype(BF16)
    dims = ((1,), (0,))
    tail = dot(high, pick, dims) + dot(low, pick, dims)
    dealt = []
    for ref in (q_ref, k_ref, v_ref, g_ref, o_ref):
        rows = ref[BULK:TOKENS, :].astype(F32)
        by_head = [deal(rows, h) for h in range(HEADS)]
        dealt.append(
            [
                jnp.stack([by_head[h][j] for h in range(HEADS)], axis=1).reshape(BULK, DIM)
                for j in range(GROUPS)
            ]
        )
    at = lax.broadcasted_iota(jnp.int32, (BULK, 128), 1)
    for j in range(GROUPS):
        total = jnp.sum(dealt[3][j] * dealt[4][j], axis=1, keepdims=True)
        tail = jnp.where(at == DOT_LANE + HEADS + j, total, tail)
    pieces = [dealt[c][j] for j in range(GROUPS) for c in range(4)]
    pieces.append(tail[:, DOT_LANE:])
    out_ref[:, 4 * WIDTH : SEND] = jnp.concatenate(pieces, axis=1).astype(BF16)


def unpack_kernel(in_ref, dq_ref, dk_ref, dv_ref):
    for c, ref in enumerate((dq_ref, dk_ref, dv_ref)):
        ref[0:BULK, :] = in_ref[:, c * WIDTH : (c + 1) * WIDTH]
        parts = []
        for j in range(GROUPS):
            start = 3 * WIDTH + (3 * j + c) * DIM
            parts.append(in_ref[:, start : start + DIM].astype(F32).reshape(8, HEADS, 8, DIM))
        heads = []
        for h in range(HEADS):
            heads.append(
                jnp.stack([parts[j][:, h] for j in range(GROUPS)], axis=1).reshape(EXTRA, DIM)
            )
        ref[BULK:TOKENS, :] = jnp.concatenate(heads, axis=1).astype(BF16)


def unit_grads(q, k, v, g, dots, q_all, g_all, masked):
    scores = dot(k, q, ((1,), (1,)))
    if masked:
        token = lax.broadcasted_iota(jnp.int32, scores.shape, 0) % 8
        other = lax.broadcasted_iota(jnp.int32, scores.shape, 1) % 8
        scores = jnp.where(token == other, scores, -1e30)
    top = jnp.max(scores, axis=0, keepdims=True)
    weights = jnp.exp2((scores - top) * EXP_SCALE)
    attend = weights * (1.0 / jnp.sum(weights, axis=0, keepdims=True))
    shifted = dot(v, g, ((1,), (1,))) - dots
    dscore = (attend * shifted).astype(BF16)
    dv = dot(attend.astype(BF16), g, ((1,), (0,)))
    dk = dot(dscore, q, ((1,), (0,)))
    dq = dot(dscore, k, ((0,), (0,)))
    return dq, dk, dv


def time_kernel(in_ref, out_ref):
    tail = in_ref[:, SEND - 128 : SEND]
    row = lax.broadcasted_iota(jnp.int32, (16, 128), 0)
    lane = lax.broadcasted_iota(jnp.int32, (16, 128), 1)
    pick = jnp.where(lane == row + DOT_LANE, 1.0, 0.0).astype(BF16)
    dots = dot(pick, tail, ((1,), (1,)))
    for unit in range(HEADS + GROUPS):
        if unit < HEADS:
            starts = [c * WIDTH + unit * DIM for c in range(4)]
            ends = [c * WIDTH + unit * DIM for c in range(3)]
        else:
            j = unit - HEADS
            starts = [4 * WIDTH + (4 * j + c) * DIM for c in range(4)]
            ends = [3 * WIDTH + (3 * j + c) * DIM for c in range(3)]
        q, k, v, g = [in_ref[:, s : s + DIM] for s in starts]
        dq, dk, dv = unit_grads(q, k, v, g, dots[unit : unit + 1, :], q, g, True)
        out_ref[:, ends[0] : ends[0] + DIM] = (dq * SCALE).astype(BF16)
        out_ref[:, ends[1] : ends[1] + DIM] = (dk * SCALE).astype(BF16)
        out_ref[:, ends[2] : ends[2] + DIM] = dv.astype(BF16)
    out_ref[:, 3 * WIDTH + 3 * GROUPS * DIM : BACK] = jnp.zeros(
        (BULK, BACK - 3 * WIDTH - 3 * GROUPS * DIM), BF16
    )


def space_kernel(q_ref, k_ref, v_ref, o_ref, g_ref, dq_ref, dk_ref, dv_ref):
    prod = g_ref[...].astype(F32) * o_ref[...].astype(F32)
    high, low = split(prod)
    row = lax.broadcasted_iota(jnp.int32, (HEADS, WIDTH), 0)
    column = lax.broadcasted_iota(jnp.int32, (HEADS, WIDTH), 1)
    inside = (column >= row * DIM) & (column < (row + 1) * DIM)
    pick = jnp.where(inside, 1.0, 0.0).astype(BF16)
    dims = ((1,), (1,))
    dots = dot(pick, high, dims) + dot(pick, low, dims)
    for h in range(HEADS):
        cols = slice(h * DIM, (h + 1) * DIM)
        k, v = k_ref[:, cols], v_ref[:, cols]
        dk_sum = dv_sum = None
        for start, size in ((0, 256), (256, 256), (512, 192)):
            rows = slice(start, start + size)
            q, g = q_ref[rows, cols], g_ref[rows, cols]
            dq, dk, dv = unit_grads(q, k, v, g, dots[h : h + 1, rows], None, None, False)
            dq_ref[rows, cols] = (dq * SCALE).astype(BF16)
            dk_sum = dk if dk_sum is None else dk_sum + dk
            dv_sum = dv if dv_sum is None else dv_sum + dv
        dk_ref[:, cols] = (dk_sum * SCALE).astype(BF16)
        dv_ref[:, cols] = dv_sum.astype(BF16)


def call(kernel, outs, cost_flops, *args):
    moved = sum(a.size * 2 for a in args) + sum(math.prod(o) * 2 for o in outs)
    return pl.pallas_call(
        kernel,
        out_shape=tuple(jax.ShapeDtypeStruct(o, BF16) for o in outs),
        compiler_params=pltpu.CompilerParams(vmem_limit_bytes=VMEM),
        cost_estimate=pl.CostEstimate(flops=cost_flops, bytes_accessed=moved, transcendentals=0),
        name=kernel.__name__,
    )(*args)


def body(sq, sk, sv, so, sg, tq, tk, tv, to, tg):
    flat = [x.reshape(TOKENS, WIDTH) for x in (sq, sk, sv, so, sg, tq, tk, tv, to, tg)]
    sq, sk, sv, so, sg, tq, tk, tv, to, tg = flat
    grad = (TOKENS, WIDTH)
    (sent,) = call(pack_kernel, [(BULK, SEND)], 10**9, tq, tk, tv, tg, to)
    got = lax.all_to_all(sent, "seq", split_axis=0, concat_axis=0, tiled=True)
    space = call(space_kernel, [grad, grad, grad], 4 * 10**10, sq, sk, sv, so, sg)
    (done,) = call(time_kernel, [(BULK, BACK)], 10**10, got)
    back = lax.all_to_all(done, "seq", split_axis=0, concat_axis=0, tiled=True)
    time = call(unpack_kernel, [grad, grad, grad], 10**9, back)
    return tuple(x.reshape(1, TOKENS, WIDTH) for x in (*space, *time))


def solution(mesh):
    spec = P(("dp", "seq"), None, None)
    return jax.shard_map(
        body, mesh=mesh, in_specs=(spec,) * 10, out_specs=(spec,) * 6, check_vma=False
    )
```

```python
import math

import jax
import jax.numpy as jnp
from jax import lax
from jax.experimental import pallas as pl
from jax.experimental.pallas import tpu as pltpu
from jax.sharding import PartitionSpec as P

HEADS = 8
DIM = 72
WIDTH = HEADS * DIM
TOKENS = 704
FRAMES = 64
BULK = 512
EXTRA = TOKENS - BULK
SEND = 200
BACK = 152
UNITS = 22
ROWS = 4 * FRAMES
TILE = DIM // 8
SCALE = 1.0 / math.sqrt(DIM)
EXP_SCALE = SCALE * math.log2(math.e)
VMEM = 50 * 1024 * 1024
BF16 = jnp.bfloat16
F32 = jnp.float32
NN = ((1,), (0,))
NT = ((1,), (1,))
TN = ((0,), (0,))


def dot(a, b, dims):
    return lax.dot_general(a, b, (dims, ((), ())), preferred_element_type=F32)


def iota(shape, axis):
    return lax.broadcasted_iota(jnp.int32, shape, axis)


def ones_where(condition):
    return jnp.where(condition, 1.0, 0.0).astype(BF16)


def roll(x, shift):
    return pltpu.roll(x, shift, x.ndim - 1)


def pack_kernel(*refs):
    main, extra, out_ref = refs[:5], refs[5:10], refs[10]
    b = pl.program_id(0)
    q, k, v, g, o = [ref[...].astype(F32) for ref in main]
    left = iota((WIDTH, 128), 1) < 64
    row = iota((EXTRA, 256), 0)
    lane = iota((EXTRA, 256), 1)
    base = 24 * (2 * b + lane // 128)
    spread = None
    for c in range(4):
        at = lane % 128 - 24 * c
        pick = ones_where((at >= 0) & (at < 24) & (row == base + at))
        part = dot(extra[c][:, :EXTRA], pick, NN)
        spread = part if spread is None else spread + part
    dots_main = jnp.sum((g * o).reshape(HEADS, DIM, 128), axis=1)
    more = extra[3][:, :EXTRA].astype(F32) * extra[4][:, :EXTRA].astype(F32)
    dots_more = jnp.sum(more.reshape(HEADS, DIM, EXTRA), axis=1)
    tail = None
    for dots, size in ((dots_main, 128), (dots_more, EXTRA)):
        shape = (HEADS, 8, size)
        kept = jnp.where(iota(shape, 2) % 4 == iota(shape, 1) % 4, dots[:, None, :], 0.0)
        token = iota((size, 256), 0)
        lane = iota((size, 256), 1)
        if size == 128:
            pick = (token // 64 == lane // 128) & ((token % 64) // 4 == lane % 128 - 96)
        else:
            at = token - 24 * (2 * b + lane // 128)
            pick = (at >= 0) & (at < 24) & (at // 4 == lane % 128 - 112)
        part = dot(kept.reshape(64, size).astype(BF16), ones_where(pick), NN)
        tail = part if tail is None else tail + part
    body_lane = iota((HEADS, 7, 8, 128), 3) < 96
    for side in range(2):
        pairs = []
        for x, y in ((q, k), (v, g)):
            joined = jnp.where(left, x, roll(y, 64)) if side == 0 else jnp.where(left, roll(x, 64), y)
            pairs.append(joined.reshape(HEADS, TILE, 8, 128))
        rest = spread[:, 128 * side : 128 * side + 128].reshape(HEADS, TILE, 8, 128)
        filler = [roll(rest[:, t], 96 - 32 * p) for t in (7, 8) for p in range(3)]
        filler.append(tail[:, 128 * side : 128 * side + 128].reshape(HEADS, 8, 128))
        rest = jnp.where(body_lane, rest[:, :7], jnp.stack(filler, axis=1))
        message = jnp.concatenate([*pairs, rest], axis=1).reshape(HEADS * SEND, 128)
        out_ref[side * HEADS * SEND : (side + 1) * HEADS * SEND, :] = message.astype(BF16)


def unpack_kernel(in_ref, *out_refs):
    b = pl.program_id(0)
    size = HEADS * BACK

    def block(a):
        start = pl.multiple_of(a * size, 16)
        return in_ref[pl.ds(start, size), :].astype(F32).reshape(HEADS, BACK // 8, 8, 128)

    @pl.when(b < 4)
    def _():
        one, two = block(2 * b), block(2 * b + 1)
        left = iota((HEADS, TILE, 8, 128), 3) < 64
        first, second = one[:, :TILE], two[:, :TILE]
        grads = (
            jnp.where(left, first, roll(second, 64)),
            jnp.where(left, roll(first, 64), second),
            jnp.where(left, one[:, TILE : 2 * TILE], roll(two[:, TILE : 2 * TILE], 64)),
        )
        for ref, grad in zip(out_refs, grads):
            ref[...] = grad.reshape(WIDTH, 128).astype(BF16)

    for step, owners in ((4, range(6)), (5, range(4, 8))):

        @pl.when(b == step)
        def _(step=step, owners=owners):
            blocks = [block(a) for a in owners]
            token = 128 * (step - 4) + iota((256, 128), 1)
            row = iota((256, 128), 0)
            sums = [None] * 3
            for i in range(0, len(blocks), 2):
                wide = [x[:, TILE : 2 * TILE].reshape(WIDTH, 128) for x in blocks[i : i + 2]]
                wide = jnp.concatenate(wide, axis=1).astype(BF16)
                at = token - 24 * (owners[i] + row // 128)
                for c in range(3):
                    inside = (at >= 0) & (at < (24, 24, 16)[c])
                    pick = ones_where(inside & (row % 128 == 64 + 24 * c + at))
                    part = dot(wide, pick, NN)
                    sums[c] = part if sums[c] is None else sums[c] + part
            left_over = jnp.stack([x[:, 2 * TILE] for x in blocks], axis=1)
            left_over = left_over.reshape(HEADS, 8 * len(blocks), 128).astype(BF16)
            shape = (8 * len(blocks), 128)
            row = iota(shape, 0)
            place = 24 * (owners[0] + row // 8) + 16 + row % 8
            pick = ones_where(128 * (step - 4) + iota(shape, 1) == place)
            last = [dot(left_over[h], pick, TN)[:DIM] for h in range(HEADS)]
            sums[2] = sums[2] + jnp.concatenate(last, axis=0)
            for ref, grad in zip(out_refs, sums):
                ref[...] = grad.astype(BF16)


def softmax_t(scores):
    top = jnp.max(scores, axis=0, keepdims=True)
    weights = jnp.exp2((scores - top) * EXP_SCALE)
    return weights * (1.0 / jnp.sum(weights, axis=0, keepdims=True))


def time_kernel(in_ref, out_ref, held, tails, grads):
    row = iota((256, 256), 0)
    order = ones_where(iota((256, 256), 1) == 128 * ((row // 4) % 2) + 4 * (row // 8) + row % 4)
    lane = iota((8, 128), 1)
    upper = iota((8, 128), 0) < 4

    def arrive(i, carry):
        start = pl.multiple_of(i * 2 * SEND, 16)
        at = pl.ds(pl.multiple_of(i * 8, 8), 8)
        x = in_ref[pl.ds(start, 2 * SEND), :].astype(F32).reshape(2, SEND // 8, 8, 128)
        rests = []
        for f in range(2):
            m = x[f, 2 * TILE :]
            ends = [
                jnp.where(
                    lane < 32,
                    roll(m[t], 32),
                    jnp.where(lane < 64, roll(m[t + 1], 64), roll(m[t + 2], 96)),
                )
                for t in (0, 3)
            ]
            rests.append(jnp.concatenate([m, ends[0][None], ends[1][None]], axis=0))
        sets = (
            (x[0, :TILE], x[1, :TILE]),
            (x[0, TILE : 2 * TILE], x[1, TILE : 2 * TILE]),
            rests,
        )
        turned = []
        for parts in sets:
            wide = jnp.concatenate([p.reshape(DIM, 128) for p in parts], axis=1).astype(BF16)
            turned.append(dot(order, wide, NT).reshape(32, 8, DIM))
        for c in range(4):
            half = turned[c // 2]
            held[c, 0:16, at, 0:DIM] = half[16 * (c % 2) : 16 * (c % 2) + 16]
            held[c, 16:UNITS, at, 0:DIM] = turned[2][6 * c : 6 * c + 6]
        tails[at, :] = jnp.where(upper, x[0, SEND // 8 - 1], x[1, SEND // 8 - 1])
        return carry

    lax.fori_loop(0, FRAMES // 2, arrive, 0, unroll=16)
    pick = ones_where(iota((32, 128), 1) == iota((32, 128), 0) + 96)
    dots = dot(pick, tails[...].astype(BF16), NT)
    same = iota((ROWS, ROWS), 0) % 4 == iota((ROWS, ROWS), 1) % 4
    for u in range(UNITS):
        q, k, v, g = [held[c, u, :, 0:DIM].astype(BF16) for c in range(4)]
        attend = softmax_t(jnp.where(same, dot(k, q, NT), -1e30))
        dscore = (attend * (dot(v, g, NT) - dots[u : u + 1, :])).astype(BF16)
        grads[0, u, :, 0:DIM] = dot(dscore, k, TN) * SCALE
        grads[1, u, :, 0:DIM] = dot(dscore, q, NN) * SCALE
        grads[2, u, :, 0:DIM] = dot(attend.astype(BF16), g, NN)

    def leave(i, carry):
        at = pl.ds(pl.multiple_of(i * 8, 8), 8)
        sets = (
            (grads[0, 0:16, at, 0:DIM], grads[1, 0:16, at, 0:DIM]),
            (
                grads[2, 0:16, at, 0:DIM],
                grads[0, 16:UNITS, at, 0:DIM],
                grads[1, 16:UNITS, at, 0:DIM],
                grads[2, 16:20, at, 0:DIM],
            ),
        )
        turned = []
        for parts in sets:
            rows = jnp.concatenate(parts, axis=0).reshape(256, DIM).astype(BF16)
            turned.append(dot(rows, order, TN))
        a = jnp.where(lane < DIM, grads[2, 20, at, :], 0.0)
        c = jnp.where(lane < DIM, grads[2, 21, at, :], 0.0)
        ends = (
            jnp.where(upper, a, pltpu.roll(c, 4, 0)),
            jnp.where(upper, pltpu.roll(a, 4, 0), c),
        )
        pieces = []
        for f in range(2):
            pieces += [t[:, 128 * f : 128 * f + 128] for t in turned] + [ends[f]]
        start = pl.multiple_of(i * 2 * BACK, 16)
        out_ref[pl.ds(start, 2 * BACK), :] = jnp.concatenate(pieces, axis=0).astype(BF16)
        return carry

    lax.fori_loop(0, FRAMES // 2, leave, 0, unroll=16)


def space_kernel(q_ref, k_ref, v_ref, o_ref, g_ref, dq_ref, dk_ref, dv_ref):
    q2, k2, v2, o2, g2 = [ref[...].astype(F32) for ref in (q_ref, k_ref, v_ref, o_ref, g_ref)]
    dots = jnp.sum((g2 * o2).reshape(2, DIM, TOKENS), axis=1)
    grads = ([], [], [])
    for h in range(2):
        part = slice(h * DIM, (h + 1) * DIM)
        q, k, v, g = [x[part].astype(BF16) for x in (q2, k2, v2, g2)]
        k_rows, v_rows = k2[part].T.astype(BF16), v2[part].T.astype(BF16)
        dq, dk, dv = [], None, None
        for start, size in ((0, 256), (256, 256), (512, 192)):
            cols = slice(start, start + size)
            attend = softmax_t(dot(k_rows, q[:, cols], NN))
            shifted = dot(v_rows, g[:, cols], NN) - dots[h : h + 1, cols]
            dscore = (attend * shifted).astype(BF16)
            dq.append(dot(k, dscore, NN))
            dk_part = dot(q[:, cols], dscore, NT)
            dv_part = dot(g[:, cols], attend.astype(BF16), NT)
            dk = dk_part if dk is None else dk + dk_part
            dv = dv_part if dv is None else dv + dv_part
        grads[0].append(jnp.concatenate(dq, axis=1) * SCALE)
        grads[1].append(dk * SCALE)
        grads[2].append(dv)
    for ref, halves in zip((dq_ref, dk_ref, dv_ref), grads):
        ref[...] = jnp.concatenate(halves, axis=0).astype(BF16)


def call(kernel, out_shapes, args, flops, **specs):
    moved = sum(a.size * 2 for a in args) + sum(math.prod(o) * 2 for o in out_shapes)
    return pl.pallas_call(
        kernel,
        out_shape=tuple(jax.ShapeDtypeStruct(o, BF16) for o in out_shapes),
        compiler_params=pltpu.CompilerParams(vmem_limit_bytes=VMEM),
        cost_estimate=pl.CostEstimate(flops=flops, bytes_accessed=moved, transcendentals=0),
        name=kernel.__name__,
        **specs,
    )(*args)


def pack(q, k, v, g, o):
    main = pl.BlockSpec((WIDTH, 128), lambda b: (0, b))
    extra = pl.BlockSpec((WIDTH, 256), lambda b: (0, 2))
    return call(
        pack_kernel,
        [(FRAMES * SEND, 128)],
        (q, k, v, g, o) * 2,
        10**9,
        grid=(4,),
        in_specs=[main] * 5 + [extra] * 5,
        out_specs=(pl.BlockSpec((16 * SEND, 128), lambda b: (b, 0)),),
    )[0]


def unpack(back):
    return call(
        unpack_kernel,
        [(WIDTH, TOKENS)] * 3,
        (back,),
        10**9,
        grid=(6,),
        in_specs=[pl.BlockSpec((FRAMES * BACK, 128), lambda b: (0, 0))],
        out_specs=(pl.BlockSpec((WIDTH, 128), lambda b: (0, b)),) * 3,
    )


def time_grads(got):
    return call(
        time_kernel,
        [(FRAMES * BACK, 128)],
        (got,),
        10**10,
        scratch_shapes=[
            pltpu.VMEM((4, UNITS, ROWS, 128), F32),
            pltpu.VMEM((ROWS, 128), F32),
            pltpu.VMEM((3, UNITS, ROWS, 128), F32),
        ],
    )[0]


def space_grads(*args):
    spec = pl.BlockSpec((2 * DIM, TOKENS), lambda b: (b, 0))
    return call(
        space_kernel,
        [(WIDTH, TOKENS)] * 3,
        args,
        4 * 10**10,
        grid=(4,),
        in_specs=[spec] * 5,
        out_specs=(spec,) * 3,
    )


def exchange(x, rows):
    x = x.reshape(FRAMES, rows, 128)
    x = lax.all_to_all(x, "seq", split_axis=0, concat_axis=0, tiled=True)
    return x.reshape(FRAMES * rows, 128)


def body(*args):
    sq, sk, sv, so, sg, tq, tk, tv, to, tg = [jnp.swapaxes(x[0], 0, 1) for x in args]
    got = exchange(pack(tq, tk, tv, tg, to), SEND)
    space = space_grads(sq, sk, sv, so, sg)
    time = unpack(exchange(time_grads(got), BACK))
    return tuple(jnp.swapaxes(x, 0, 1)[None] for x in (*space, *time))


def solution(mesh):
    spec = P(("dp", "seq"), None, None)
    return jax.shard_map(
        body, mesh=mesh, in_specs=(spec,) * 10, out_specs=(spec,) * 6, check_vma=False
    )
```

```python
import math

import jax
import jax.numpy as jnp
from jax import lax
from jax.experimental import pallas as pl
from jax.experimental.pallas import tpu as pltpu
from jax.sharding import PartitionSpec as P

HEADS = 8
DIM = 72
WIDTH = HEADS * DIM
TOKENS = 704
FRAMES = 64
BULK = 512
EXTRA = TOKENS - BULK
SEND = 200
BACK = 152
UNITS = 22
ROWS = 4 * FRAMES
TILE = DIM // 8
SCALE = 1.0 / math.sqrt(DIM)
EXP_SCALE = SCALE * math.log2(math.e)
BF16 = jnp.bfloat16
F32 = jnp.float32
NN = ((1,), (0,))
NT = ((1,), (1,))
TN = ((0,), (0,))


def dot(a, b, dims):
    return lax.dot_general(a, b, (dims, ((), ())), preferred_element_type=F32)


def iota(shape, axis):
    return lax.broadcasted_iota(jnp.int32, shape, axis)


def ones_where(condition):
    return jnp.where(condition, 1.0, 0.0).astype(BF16)


def roll(x, shift):
    return pltpu.roll(x, shift, x.ndim - 1)


def pack_kernel(q_ref, k_ref, v_ref, g_ref, o_ref, out_ref, picks, dot_pick):
    @pl.when(pl.program_id(0) == 0)
    def _():
        shape = (EXTRA, 128)
        row, lane = iota(shape, 0), iota(shape, 1)
        for a in range(8):
            at = row - 24 * a
            mine = (at >= 0) & (at < 24)
            cols = slice(128 * a, 128 * a + 128)
            for c in range(4):
                picks[c, :, cols] = ones_where(mine & (lane == at + 24 * c))
            dot_pick[:, cols] = ones_where(mine & (lane == 112 + at // 4))

    refs = (q_ref, k_ref, v_ref, g_ref)
    q, k, v, g = [ref[:, :BULK].astype(F32) for ref in refs]
    spread = None
    for c in range(4):
        part = dot(refs[c][:, BULK:], picks[c], NN)
        spread = part if spread is None else spread + part
    prod = g_ref[...].astype(F32) * o_ref[...].astype(F32)
    dots = jnp.sum(prod.reshape(2, DIM, TOKENS), axis=1)
    shape = (2, 8, TOKENS)
    kept = jnp.where(iota(shape, 2) % 4 == iota(shape, 1) % 4, dots[:, None, :], 0.0)
    kept = kept.reshape(16, TOKENS).astype(BF16)
    token, lane = iota((128, 256), 0), iota((128, 256), 1)
    pick = (token // 64 == lane // 128) & ((token % 64) // 4 == lane % 128 - 96)
    stacked = jnp.concatenate([kept[:, 128 * b : 128 * b + 128] for b in range(4)], axis=0)
    tail = dot(stacked, ones_where(pick), NN)
    tail_more = dot(kept[:, BULK:], dot_pick[...], NN)
    left = iota((2 * DIM, 128), 1) < 64
    body_lane = iota((2, 7, 8, 128), 3) < 96
    for a in range(8):
        b, odd = a // 2, a % 2
        cols = slice(128 * b, 128 * b + 128)
        pairs = []
        for x, y in ((q[:, cols], k[:, cols]), (v[:, cols], g[:, cols])):
            joined = jnp.where(left, roll(x, 64), y) if odd else jnp.where(left, x, roll(y, 64))
            pairs.append(joined.reshape(2, TILE, 8, 128))
        cols = slice(128 * a, 128 * a + 128)
        rest = spread[:, cols].reshape(2, TILE, 8, 128)
        filler = [roll(rest[:, t], 96 - 32 * p) for t in (7, 8) for p in range(3)]
        here = tail[16 * b : 16 * b + 16, 128 * odd : 128 * odd + 128] + tail_more[:, cols]
        filler.append(here.reshape(2, 8, 128))
        rest = jnp.where(body_lane, rest[:, :7], jnp.stack(filler, axis=1))
        message = jnp.concatenate([*pairs, rest], axis=1).reshape(2 * SEND, 128)
        out_ref[a] = message.astype(BF16)


def unpack_kernel(in_ref, dq_ref, dk_ref, dv_ref, picks, end_pick):
    @pl.when(pl.program_id(0) == 0)
    def _():
        shape = (128, EXTRA)
        row, token = iota(shape, 0), iota(shape, 1)
        for a in range(8):
            at = token - 24 * a
            for c in range(3):
                mine = (at >= 0) & (at < (24, 24, 16)[c]) & (row == 64 + 24 * c + at)
                rows = slice(128 * (a % 2), 128 * (a % 2) + 128)
                picks[a // 2, rows, 256 * c : 256 * c + EXTRA] = ones_where(mine)
                picks[a // 2, rows, 256 * c + EXTRA : 256 * c + 256] = jnp.zeros((128, 64), BF16)
        shape = (64, EXTRA)
        row = iota(shape, 0)
        end_pick[...] = ones_where(iota(shape, 1) == 24 * (row // 8) + 16 + row % 8)

    left = iota((2, TILE, 8, 128), 3) < 64
    more, ends = None, []
    for b in range(4):
        one, two = [
            in_ref[a].astype(F32).reshape(2, BACK // 8, 8, 128) for a in (2 * b, 2 * b + 1)
        ]
        cols = slice(128 * b, 128 * b + 128)
        first, second = one[:, :TILE], two[:, :TILE]
        third, fourth = one[:, TILE : 2 * TILE], two[:, TILE : 2 * TILE]
        grads = (
            jnp.where(left, first, roll(second, 64)),
            jnp.where(left, roll(first, 64), second),
            jnp.where(left, third, roll(fourth, 64)),
        )
        for ref, grad in zip((dq_ref, dk_ref, dv_ref), grads):
            ref[:, cols] = grad.reshape(2 * DIM, 128).astype(BF16)
        wide = jnp.concatenate([x.reshape(2 * DIM, 128) for x in (third, fourth)], axis=1)
        part = dot(wide.astype(BF16), picks[b], NN)
        more = part if more is None else more + part
        ends += [one[:, 2 * TILE], two[:, 2 * TILE]]
    ends = jnp.stack(ends, axis=1).reshape(2, 64, 128).astype(BF16)
    last = [dot(ends[h], end_pick[...], TN)[:DIM] for h in range(2)]
    for c, ref in enumerate((dq_ref, dk_ref, dv_ref)):
        grad = more[:, 256 * c : 256 * c + EXTRA]
        if c == 2:
            grad = grad + jnp.concatenate(last, axis=0)
        ref[:, BULK:] = grad.astype(BF16)


def softmax_t(scores):
    top = jnp.max(scores, axis=0, keepdims=True)
    weights = jnp.exp2((scores - top) * EXP_SCALE)
    return weights * (1.0 / jnp.sum(weights, axis=0, keepdims=True))


def time_kernel(in_ref, out_ref, held, tails, grads):
    row = iota((256, 256), 0)
    order = ones_where(iota((256, 256), 1) == 128 * ((row // 4) % 2) + 4 * (row // 8) + row % 4)
    lane = iota((8, 128), 1)
    upper = iota((8, 128), 0) < 4

    def arriving(i):
        start = pl.multiple_of(i * 2 * SEND, 16)
        x = in_ref[pl.ds(start, 2 * SEND), :].astype(F32).reshape(2, SEND // 8, 8, 128)
        rests = []
        for f in range(2):
            m = x[f, 2 * TILE :]
            ends = [
                jnp.where(
                    lane < 32,
                    roll(m[t], 32),
                    jnp.where(lane < 64, roll(m[t + 1], 64), roll(m[t + 2], 96)),
                )
                for t in (0, 3)
            ]
            rests.append(jnp.concatenate([m, ends[0][None], ends[1][None]], axis=0))
        sets = (
            (x[0, :TILE], x[1, :TILE]),
            (x[0, TILE : 2 * TILE], x[1, TILE : 2 * TILE]),
            rests,
        )
        turned = []
        for parts in sets:
            wide = jnp.concatenate([p.reshape(DIM, 128) for p in parts], axis=1).astype(BF16)
            turned.append(dot(order, wide, NT).reshape(32, 8, DIM))
        return turned, jnp.where(upper, x[0, SEND // 8 - 1], x[1, SEND // 8 - 1])

    def keep(i, turned, tail):
        at = pl.ds(pl.multiple_of(i * 8, 8), 8)
        for c in range(4):
            half = turned[c // 2]
            held[c, 0:16, at, 0:DIM] = half[16 * (c % 2) : 16 * (c % 2) + 16]
            held[c, 16:UNITS, at, 0:DIM] = turned[2][6 * c : 6 * c + 6]
        tails[at, :] = tail

    ahead(FRAMES // 2, arriving, keep)
    pick = ones_where(iota((32, 128), 1) == iota((32, 128), 0) + 96)
    dots = dot(pick, tails[...].astype(BF16), NT)
    same = iota((ROWS, ROWS), 0) % 4 == iota((ROWS, ROWS), 1) % 4

    def load(u):
        q, k, v, g = [held[c, u, :, 0:DIM].astype(BF16) for c in range(4)]
        return q, k, g, dot(k, q, NT), dot(v, g, NT)

    following = load(0)
    for u in range(UNITS):
        q, k, g, scores, grad_attend = following
        if u + 1 < UNITS:
            following = load(u + 1)
        attend = softmax_t(jnp.where(same, scores, -1e30))
        dscore = (attend * (grad_attend - dots[u : u + 1, :])).astype(BF16)
        grads[0, u, :, 0:DIM] = dot(dscore, k, TN) * SCALE
        grads[1, u, :, 0:DIM] = dot(dscore, q, NN) * SCALE
        grads[2, u, :, 0:DIM] = dot(attend.astype(BF16), g, NN)

    def leaving(i):
        at = pl.ds(pl.multiple_of(i * 8, 8), 8)
        sets = (
            (grads[0, 0:16, at, 0:DIM], grads[1, 0:16, at, 0:DIM]),
            (
                grads[2, 0:16, at, 0:DIM],
                grads[0, 16:UNITS, at, 0:DIM],
                grads[1, 16:UNITS, at, 0:DIM],
                grads[2, 16:20, at, 0:DIM],
            ),
        )
        turned = []
        for parts in sets:
            rows = jnp.concatenate(parts, axis=0).reshape(256, DIM).astype(BF16)
            turned.append(dot(rows, order, TN))
        a = jnp.where(lane < DIM, grads[2, 20, at, :], 0.0)
        c = jnp.where(lane < DIM, grads[2, 21, at, :], 0.0)
        ends = (
            jnp.where(upper, a, pltpu.roll(c, 4, 0)),
            jnp.where(upper, pltpu.roll(a, 4, 0), c),
        )
        return turned, ends

    def send(i, turned, ends):
        pieces = []
        for f in range(2):
            pieces += [t[:, 128 * f : 128 * f + 128] for t in turned] + [ends[f]]
        start = pl.multiple_of(i * 2 * BACK, 16)
        out_ref[pl.ds(start, 2 * BACK), :] = jnp.concatenate(pieces, axis=0).astype(BF16)

    ahead(FRAMES // 2, leaving, send)


def ahead(count, make, use, block=16):
    def step(j, carry):
        made = make(j * block)
        for t in range(block):
            following = make(j * block + t + 1) if t + 1 < block else None
            use(j * block + t, *made)
            made = following
        return carry

    lax.fori_loop(0, count // block, step, 0)


def space_kernel(q_ref, k_ref, v_ref, o_ref, g_ref, dq_ref, dk_ref, dv_ref):
    q2, k2, v2, o2, g2 = [ref[...].astype(F32) for ref in (q_ref, k_ref, v_ref, o_ref, g_ref)]
    dots = jnp.sum((g2 * o2).reshape(2, DIM, TOKENS), axis=1)
    grads = ([], [], [])
    for h in range(2):
        part = slice(h * DIM, (h + 1) * DIM)
        q, k, v, g = [x[part].astype(BF16) for x in (q2, k2, v2, g2)]
        k_rows, v_rows = k2[part].T.astype(BF16), v2[part].T.astype(BF16)
        dq, dk, dv = [], None, None
        for start, size in ((0, 256), (256, 256), (512, 192)):
            cols = slice(start, start + size)
            attend = softmax_t(dot(k_rows, q[:, cols], NN))
            shifted = dot(v_rows, g[:, cols], NN) - dots[h : h + 1, cols]
            dscore = (attend * shifted).astype(BF16)
            dq.append(dot(k, dscore, NN))
            dk_part = dot(q[:, cols], dscore, NT)
            dv_part = dot(g[:, cols], attend.astype(BF16), NT)
            dk = dk_part if dk is None else dk + dk_part
            dv = dv_part if dv is None else dv + dv_part
        grads[0].append(jnp.concatenate(dq, axis=1) * SCALE)
        grads[1].append(dk * SCALE)
        grads[2].append(dv)
    for ref, halves in zip((dq_ref, dk_ref, dv_ref), grads):
        ref[...] = jnp.concatenate(halves, axis=0).astype(BF16)


def call(kernel, out_shapes, args, flops, vmem, **specs):
    moved = sum(a.size * 2 for a in args) + sum(math.prod(o) * 2 for o in out_shapes)
    return pl.pallas_call(
        kernel,
        out_shape=tuple(jax.ShapeDtypeStruct(o, BF16) for o in out_shapes),
        compiler_params=pltpu.CompilerParams(vmem_limit_bytes=vmem * 1024 * 1024),
        cost_estimate=pl.CostEstimate(flops=flops, bytes_accessed=moved, transcendentals=0),
        name=kernel.__name__,
        **specs,
    )(*args)


HEAD_PAIR = pl.BlockSpec((2 * DIM, TOKENS), lambda p: (p, 0))


def pack(q, k, v, g, o):
    (sent,) = call(
        pack_kernel,
        [(8, HEADS * SEND, 128)],
        (q, k, v, g, o),
        10**9,
        60,
        grid=(4,),
        in_specs=[HEAD_PAIR] * 5,
        out_specs=(pl.BlockSpec((8, 2 * SEND, 128), lambda p: (0, p, 0)),),
        scratch_shapes=[pltpu.VMEM((4, EXTRA, 1024), BF16), pltpu.VMEM((EXTRA, 1024), BF16)],
    )
    return sent


def unpack(back):
    return call(
        unpack_kernel,
        [(WIDTH, TOKENS)] * 3,
        (back.reshape(8, HEADS * BACK, 128),),
        10**9,
        50,
        grid=(4,),
        in_specs=[pl.BlockSpec((8, 2 * BACK, 128), lambda p: (0, p, 0))],
        out_specs=(HEAD_PAIR,) * 3,
        scratch_shapes=[pltpu.VMEM((4, 256, 768), BF16), pltpu.VMEM((64, EXTRA), BF16)],
    )


def time_grads(got):
    return call(
        time_kernel,
        [(FRAMES * BACK, 128)],
        (got,),
        10**10,
        50,
        scratch_shapes=[
            pltpu.VMEM((4, UNITS, ROWS, 128), F32),
            pltpu.VMEM((ROWS, 128), F32),
            pltpu.VMEM((3, UNITS, ROWS, 128), F32),
        ],
    )[0]


def space_grads(*args):
    return call(
        space_kernel,
        [(WIDTH, TOKENS)] * 3,
        args,
        4 * 10**10,
        60,
        grid=(4,),
        in_specs=[HEAD_PAIR] * 5,
        out_specs=(HEAD_PAIR,) * 3,
    )


def exchange(x, rows):
    x = x.reshape(FRAMES, rows, 128)
    x = lax.all_to_all(x, "seq", split_axis=0, concat_axis=0, tiled=True)
    return x.reshape(FRAMES * rows, 128)


def body(*args):
    sq, sk, sv, so, sg, tq, tk, tv, to, tg = [jnp.swapaxes(x[0], 0, 1) for x in args]
    got = exchange(pack(tq, tk, tv, tg, to), SEND)
    space = space_grads(sq, sk, sv, so, sg)
    time = unpack(exchange(time_grads(got), BACK))
    return tuple(jnp.swapaxes(x, 0, 1)[None] for x in (*space, *time))


def solution(mesh):
    spec = P(("dp", "seq"), None, None)
    return jax.shard_map(
        body, mesh=mesh, in_specs=(spec,) * 10, out_specs=(spec,) * 6, check_vma=False
    )
```

```python
import math

import jax
import jax.numpy as jnp
from jax import lax
from jax.experimental import pallas as pl
from jax.experimental.pallas import tpu as pltpu
from jax.sharding import PartitionSpec as P

HEADS = 8
DIM = 72
WIDTH = HEADS * DIM
TOKENS = 704
FRAMES = 64
BULK = 512
EXTRA = TOKENS - BULK
SEND = 200
BACK = 152
UNITS = 22
ROWS = 4 * FRAMES
TILE = DIM // 8
SCALE = 1.0 / math.sqrt(DIM)
EXP_SCALE = SCALE * math.log2(math.e)
BF16 = jnp.bfloat16
F32 = jnp.float32
NN = ((1,), (0,))
NT = ((1,), (1,))
TN = ((0,), (0,))


def dot(a, b, dims):
    return lax.dot_general(a, b, (dims, ((), ())), preferred_element_type=F32)


def iota(shape, axis):
    return lax.broadcasted_iota(jnp.int32, shape, axis)


def ones_where(condition):
    return jnp.where(condition, 1.0, 0.0).astype(BF16)


def roll(x, shift):
    return pltpu.roll(x, shift, x.ndim - 1)


def turn(x, shift):
    return roll(x, shift % 128) if shift % 128 else x


def pack_kernel(q_ref, k_ref, v_ref, g_ref, o_ref, out_ref, held, made, dot_pick, in_sem, out_sem):
    refs = (q_ref, k_ref, v_ref, g_ref, o_ref)

    def fetch(c, p):
        rows = pl.ds(pl.multiple_of(p * 2 * DIM, 16), 2 * DIM)
        return pltpu.make_async_copy(refs[c].at[rows, :], held.at[c, p], in_sem.at[c, p])

    def send(p):
        rows = pl.ds(pl.multiple_of(p * 2 * SEND, 16), 2 * SEND)
        return pltpu.make_async_copy(made.at[p], out_ref.at[:, rows, :], out_sem.at[p])

    for p in range(4):
        for c in range(5):
            fetch(c, p).start()

    row, lane = iota((EXTRA, 128), 0), iota((EXTRA, 128), 1)
    for a in range(8):
        at = row - 24 * a
        mine = (at >= 0) & (at < 24) & (lane == 112 + at // 4)
        dot_pick[:, 128 * a : 128 * a + 128] = ones_where(mine)
    token, lane = iota((128, 256), 0), iota((128, 256), 1)
    pick = (token // 64 == lane // 128) & ((token % 64) // 4 == lane % 128 - 96)
    pick = ones_where(pick)
    lane = iota((2 * DIM, 128), 1)
    body_lane = iota((2, 7, 8, 128), 3) < 96
    shape = (2, 8, TOKENS)
    same = iota(shape, 2) % 4 == iota(shape, 1) % 4

    def head_pair(p, carry):
        for c in range(5):
            fetch(c, p).wait()
        full = [held[c, p].astype(F32) for c in range(4)]
        dots = jnp.sum((full[3] * held[4, p].astype(F32)).reshape(2, DIM, TOKENS), axis=1)
        kept = jnp.where(same, dots[:, None, :], 0.0).reshape(16, TOKENS).astype(BF16)
        stacked = jnp.concatenate([kept[:, 128 * b : 128 * b + 128] for b in range(4)], axis=0)
        tail = dot(stacked, pick, NN)
        tail_more = dot(kept[:, BULK:], dot_pick[...], NN)
        fourth = [x[:, BULK : BULK + 128] for x in full]
        blank = jnp.zeros((2 * DIM, 64), F32)
        fifth = [jnp.concatenate([x[:, BULK + 128 :], blank], axis=1) for x in full]
        across = [jnp.where(lane < 16, x, y) for x, y in zip(fifth, fourth)]

        def gather(a):
            b, odd = a // 2, a % 2
            cols = slice(128 * b, 128 * b + 128)
            q, k, v, g = [x[:, cols] for x in full]
            pairs = []
            for x, y in ((q, k), (v, g)):
                if odd:
                    joined = jnp.where(lane < 64, roll(x, 64), y)
                else:
                    joined = jnp.where(lane < 64, x, roll(y, 64))
                pairs.append(joined.reshape(2, TILE, 8, 128))
            source = fourth if a < 5 else across if a == 5 else fifth
            moved = [turn(x, 24 * c - 24 * a) for c, x in enumerate(source)]
            rest = moved[3]
            for c in (2, 1, 0):
                rest = jnp.where(lane < 24 * c + 24, moved[c], rest)
            return pairs, rest.reshape(2, TILE, 8, 128)

        def fold(a, pairs, rest):
            b, odd = a // 2, a % 2
            filler = [turn(rest[:, t], 96 - 32 * n) for t in (7, 8) for n in range(3)]
            here = tail[16 * b : 16 * b + 16, 128 * odd : 128 * odd + 128]
            here = here + tail_more[:, 128 * a : 128 * a + 128]
            filler.append(here.reshape(2, 8, 128))
            return pairs, rest[:, :7], jnp.stack(filler, axis=1)

        def store(a, pairs, rest, filler):
            rest = jnp.where(body_lane, rest, filler)
            message = jnp.concatenate([*pairs, rest], axis=1).reshape(2 * SEND, 128)
            made[p, a] = message.astype(BF16)

        first, second = {}, {}
        for t in range(10):
            if t % 2 == 0 and t < 8:
                first[t], first[t + 1] = gather(t), gather(t + 1)
            if 1 <= t < 9:
                second[t - 1] = fold(t - 1, *first.pop(t - 1))
            if t >= 2:
                store(t - 2, *second.pop(t - 2))
        send(p).start()
        return carry

    lax.fori_loop(0, 4, head_pair, 0)
    for p in range(4):
        send(p).wait()


def unpack_kernel(in_ref, dq_ref, dk_ref, dv_ref):
    out_refs = (dq_ref, dk_ref, dv_ref)
    left = iota((2, TILE, 8, 128), 3) < 64
    lane = iota((2 * DIM, 128), 1)
    row = iota((64, 256), 0)
    end_pick = ones_where(iota((64, 256), 1) == 24 * (row // 8) + 16 + row % 8)
    seconds, ends = [], []

    def gather(b):
        one, two = [
            in_ref[a].astype(F32).reshape(2, BACK // 8, 8, 128) for a in (2 * b, 2 * b + 1)
        ]
        first, second = one[:, :TILE], two[:, :TILE]
        third, fourth = one[:, TILE : 2 * TILE], two[:, TILE : 2 * TILE]
        seconds.extend([third.reshape(2 * DIM, 128), fourth.reshape(2 * DIM, 128)])
        ends.extend([one[:, 2 * TILE], two[:, 2 * TILE]])
        return (
            jnp.where(left, first, roll(second, 64)),
            jnp.where(left, roll(first, 64), second),
            jnp.where(left, third, roll(fourth, 64)),
        )

    def store(b, grads):
        for ref, grad in zip(out_refs, grads):
            ref[:, 128 * b : 128 * b + 128] = grad.reshape(2 * DIM, 128).astype(BF16)

    def shift(c):
        return [turn(x, 24 * a - 64 - 24 * c) for a, x in enumerate(seconds)]

    def join(c, moved):
        for tile, owners in ((0, range(6)), (1, range(5, 8))):
            total = last[:, 128 * tile : 128 * tile + 128]
            for a in owners:
                at = lane - (24 * a - 128 * tile)
                mine = (at >= 0) & (at < (24, 24, 16)[c])
                total = jnp.where(mine, moved[a], total)
            start = BULK + 128 * tile
            part = total[:, : 128 - 64 * tile].astype(BF16)
            out_refs[c][:, start : start + 128 - 64 * tile] = part

    ready = gather(0)
    for b in range(4):
        following = gather(b + 1) if b < 3 else None
        store(b, ready)
        ready = following
    ends = jnp.stack(ends, axis=1).reshape(2, 64, 128).astype(BF16)
    last = [dot(ends[h], end_pick, TN)[:DIM] for h in range(2)]
    last = jnp.concatenate(last, axis=0)
    ready = shift(0)
    for c in range(3):
        following = shift(c + 1) if c < 2 else None
        join(c, ready)
        ready = following


def softmax_t(scores):
    top = jnp.max(scores, axis=0, keepdims=True)
    weights = jnp.exp2((scores - top) * EXP_SCALE)
    return weights * (1.0 / jnp.sum(weights, axis=0, keepdims=True))


def time_kernel(in_ref, out_ref, held, tails, grads, made, sem):
    row = iota((256, 256), 0)
    order = ones_where(iota((256, 256), 1) == 128 * ((row // 4) % 2) + 4 * (row // 8) + row % 4)
    unit = ones_where(iota((DIM, DIM), 0) == iota((DIM, DIM), 1))
    lane = iota((8, 128), 1)
    upper = iota((8, 128), 0) < 4

    def arriving(j):
        firsts, rests, last = [], [], []
        for p in range(2):
            start = pl.multiple_of((2 * j + p) * 2 * SEND, 16)
            x = in_ref[pl.ds(start, 2 * SEND), :].astype(F32).reshape(2, SEND // 8, 8, 128)
            sides, more = [], []
            for f in range(2):
                sides.append(jnp.concatenate([x[f, :16], x[f, TILE:]], axis=0).reshape(256, 128))
                m = x[f, 2 * TILE :]
                ends = [
                    jnp.where(
                        lane < 32,
                        roll(m[t], 32),
                        jnp.where(lane < 64, roll(m[t + 1], 64), roll(m[t + 2], 96)),
                    )
                    for t in (0, 3)
                ]
                more.append(jnp.concatenate([m, ends[0][None], ends[1][None], m], axis=0))
            wide = jnp.concatenate(sides, axis=1).astype(BF16)
            firsts.append(dot(order, wide, NT))
            rests.append(jnp.concatenate([y.reshape(128, 128) for y in more], axis=1))
            last.append(jnp.where(upper, x[0, SEND // 8 - 1], x[1, SEND // 8 - 1]))
        rest = jnp.concatenate(rests, axis=0).astype(BF16)
        return firsts, dot(order[: 8 * 4 * 6], rest, NT), last

    def keep(j, firsts, rest, last):
        for p in range(2):
            at = pl.ds(pl.multiple_of((2 * j + p) * 8, 8), 8)
            for c in range(4):
                start = 128 * (c // 2)
                half = firsts[p][128 * (c % 2) : 128 * (c % 2) + 128, start : start + DIM]
                held[c, 0:16, at, 0:DIM] = half.reshape(16, 8, DIM)
                half = rest[48 * c : 48 * c + 48, 128 * p : 128 * p + DIM]
                held[c, 16:UNITS, at, 0:DIM] = half.reshape(6, 8, DIM)
            tails[at, :] = last[p]

    ahead(0, FRAMES // 4, 8, arriving, keep)
    pick = ones_where(iota((32, 128), 1) == iota((32, 128), 0) + 96)
    dots = dot(pick, tails[...].astype(BF16), NT)
    same = iota((ROWS, ROWS), 0) % 4 == iota((ROWS, ROWS), 1) % 4

    def load(u):
        q, k, v, g = [held[c, u, :, 0:DIM].astype(BF16) for c in range(4)]
        return q, k, g, dot(k, q, NT), dot(v, g, NT)

    following = load(0)
    for u in range(UNITS):
        q, k, g, scores, grad_attend = following
        if u + 1 < UNITS:
            following = load(u + 1)
        attend = softmax_t(jnp.where(same, scores, -1e30))
        dscore = (attend * (grad_attend - dots[u : u + 1, :])).astype(BF16)
        grads[0, u, :, 0:DIM] = dot(dscore, k, TN) * SCALE
        grads[1, u, :, 0:DIM] = dot(dscore, q, NN) * SCALE
        grads[2, u, :, 0:DIM] = dot(attend.astype(BF16), g, NN)

    def swap(x):
        pairs = x.reshape(x.shape[0] // 2, 2, 8, 128)
        even, odd = pairs[:, 0], pairs[:, 1]
        first = jnp.where(upper, even, pltpu.roll(odd, 4, 1))
        second = jnp.where(upper, pltpu.roll(even, 4, 1), odd)
        return first, second

    def leaving(i):
        at = pl.ds(pl.multiple_of(i * 8, 8), 8)
        sets = (
            (grads[0, 0:16, at, :], grads[1, 0:16, at, :]),
            (
                grads[2, 0:16, at, :],
                grads[0, 16:UNITS, at, :],
                grads[1, 16:UNITS, at, :],
                grads[2, 16:20, at, :],
            ),
        )
        turned = []
        for parts in sets:
            rows = jnp.concatenate(swap(jnp.concatenate(parts, axis=0)), axis=0)
            rows = rows.reshape(256, 128)[:, :DIM].astype(BF16)
            turned.append(dot(unit, rows, NT))
        ends = swap(jnp.where(lane < DIM, grads[2, 20:22, at, :], 0.0))
        return turned, ends

    def place(i, turned, ends):
        pieces = []
        for f in range(2):
            pieces += [t[:, 128 * f : 128 * f + 128] for t in turned] + [ends[f][0]]
        start = pl.multiple_of(i * 2 * BACK, 16)
        made[pl.ds(start, 2 * BACK), :] = jnp.concatenate(pieces, axis=0).astype(BF16)

    def send(part):
        rows = pl.ds(part * FRAMES * BACK // 2, FRAMES * BACK // 2)
        return pltpu.make_async_copy(made.at[rows, :], out_ref.at[rows, :], sem.at[part])

    for part in range(2):
        ahead(part, FRAMES // 4, 16, leaving, place)
        send(part).start()
    for part in range(2):
        send(part).wait()


def ahead(part, count, block, make, use):
    def step(j, carry):
        base = part * count + j * block
        ready = make(base)
        for t in range(block):
            following = make(base + t + 1) if t + 1 < block else None
            use(base + t, *ready)
            ready = following
        return carry

    lax.fori_loop(0, count // block, step, 0)


def space_kernel(q_ref, k_ref, v_ref, o_ref, g_ref, dq_ref, dk_ref, dv_ref):
    q2, k2, v2, o2, g2 = [ref[...].astype(F32) for ref in (q_ref, k_ref, v_ref, o_ref, g_ref)]
    dots = jnp.sum((g2 * o2).reshape(2, DIM, TOKENS), axis=1)
    grads = ([], [], [])
    for h in range(2):
        part = slice(h * DIM, (h + 1) * DIM)
        q, k, v, g = [x[part].astype(BF16) for x in (q2, k2, v2, g2)]
        k_rows, v_rows = k2[part].T.astype(BF16), v2[part].T.astype(BF16)
        dq, dk, dv = [], None, None
        for start, size in ((0, 256), (256, 256), (512, 192)):
            cols = slice(start, start + size)
            attend = softmax_t(dot(k_rows, q[:, cols], NN))
            shifted = dot(v_rows, g[:, cols], NN) - dots[h : h + 1, cols]
            dscore = (attend * shifted).astype(BF16)
            dq.append(dot(k, dscore, NN))
            dk_part = dot(q[:, cols], dscore, NT)
            dv_part = dot(g[:, cols], attend.astype(BF16), NT)
            dk = dk_part if dk is None else dk + dk_part
            dv = dv_part if dv is None else dv + dv_part
        grads[0].append(jnp.concatenate(dq, axis=1) * SCALE)
        grads[1].append(dk * SCALE)
        grads[2].append(dv)
    for ref, halves in zip((dq_ref, dk_ref, dv_ref), grads):
        ref[...] = jnp.concatenate(halves, axis=0).astype(BF16)


def call(kernel, out_shapes, args, flops, vmem, **specs):
    moved = sum(a.size * 2 for a in args) + sum(math.prod(o) * 2 for o in out_shapes)
    return pl.pallas_call(
        kernel,
        out_shape=tuple(jax.ShapeDtypeStruct(o, BF16) for o in out_shapes),
        compiler_params=pltpu.CompilerParams(vmem_limit_bytes=vmem * 1024 * 1024),
        cost_estimate=pl.CostEstimate(flops=flops, bytes_accessed=moved, transcendentals=0),
        name=kernel.__name__,
        **specs,
    )(*args)


HEAD_PAIR = pl.BlockSpec((2 * DIM, TOKENS), lambda p: (p, 0))


def pack(q, k, v, g, o):
    (sent,) = call(
        pack_kernel,
        [(8, HEADS * SEND, 128)],
        (q, k, v, g, o),
        10**9,
        60,
        in_specs=[pl.BlockSpec(memory_space=pltpu.HBM)] * 5,
        out_specs=(pl.BlockSpec(memory_space=pltpu.HBM),),
        scratch_shapes=[
            pltpu.VMEM((5, 4, 2 * DIM, TOKENS), BF16),
            pltpu.VMEM((4, 8, 2 * SEND, 128), BF16),
            pltpu.VMEM((EXTRA, 1024), BF16),
            pltpu.SemaphoreType.DMA((5, 4)),
            pltpu.SemaphoreType.DMA((4,)),
        ],
    )
    return sent


def unpack(back):
    return call(
        unpack_kernel,
        [(WIDTH, TOKENS)] * 3,
        (back.reshape(8, HEADS * BACK, 128),),
        10**9,
        50,
        grid=(4,),
        in_specs=[pl.BlockSpec((8, 2 * BACK, 128), lambda p: (0, p, 0))],
        out_specs=(HEAD_PAIR,) * 3,
    )


def time_grads(got):
    return call(
        time_kernel,
        [(FRAMES * BACK, 128)],
        (got,),
        10**10,
        50,
        in_specs=[pl.BlockSpec(memory_space=pltpu.VMEM)],
        out_specs=(pl.BlockSpec(memory_space=pltpu.HBM),),
        scratch_shapes=[
            pltpu.VMEM((4, UNITS, ROWS, 128), F32),
            pltpu.VMEM((ROWS, 128), F32),
            pltpu.VMEM((3, UNITS, ROWS, 128), F32),
            pltpu.VMEM((FRAMES * BACK, 128), BF16),
            pltpu.SemaphoreType.DMA((2,)),
        ],
    )[0]


def space_grads(*args):
    return call(
        space_kernel,
        [(WIDTH, TOKENS)] * 3,
        args,
        4 * 10**10,
        60,
        grid=(4,),
        in_specs=[HEAD_PAIR] * 5,
        out_specs=(HEAD_PAIR,) * 3,
    )


def exchange(x, rows):
    x = x.reshape(FRAMES, rows, 128)
    x = lax.all_to_all(x, "seq", split_axis=0, concat_axis=0, tiled=True)
    return x.reshape(FRAMES * rows, 128)


def body(*args):
    sq, sk, sv, so, sg, tq, tk, tv, to, tg = [jnp.swapaxes(x[0], 0, 1) for x in args]
    got = exchange(pack(tq, tk, tv, tg, to), SEND)
    space = space_grads(sq, sk, sv, so, sg)
    time = unpack(exchange(time_grads(got), BACK))
    return tuple(jnp.swapaxes(x, 0, 1)[None] for x in (*space, *time))


def solution(mesh):
    spec = P(("dp", "seq"), None, None)
    return jax.shard_map(
        body, mesh=mesh, in_specs=(spec,) * 10, out_specs=(spec,) * 6, check_vma=False
    )
```

```python
import math

import jax
import jax.numpy as jnp
from jax import lax
from jax.experimental import pallas as pl
from jax.experimental.pallas import tpu as pltpu
from jax.sharding import PartitionSpec as P

HEADS = 8
DIM = 72
WIDTH = HEADS * DIM
TOKENS = 704
FRAMES = 64
BULK = 512
EXTRA = TOKENS - BULK
SEND = 200
BACK = 152
UNITS = 22
ROWS = 4 * FRAMES
TILE = DIM // 8
SCALE = 1.0 / math.sqrt(DIM)
EXP_SCALE = SCALE * math.log2(math.e)
BF16 = jnp.bfloat16
F32 = jnp.float32
NN = ((1,), (0,))
NT = ((1,), (1,))
TN = ((0,), (0,))


def dot(a, b, dims):
    return lax.dot_general(a, b, (dims, ((), ())), preferred_element_type=F32)


def iota(shape, axis):
    return lax.broadcasted_iota(jnp.int32, shape, axis)


def ones_where(condition):
    return jnp.where(condition, 1.0, 0.0).astype(BF16)


def roll(x, shift):
    return pltpu.roll(x, shift, x.ndim - 1)


def turn(x, shift):
    return roll(x, shift % 128) if shift % 128 else x


def pack_kernel(q_ref, k_ref, v_ref, g_ref, o_ref, out_ref, held, made, picks, dot_pick, in_sem, out_sem):
    refs = (q_ref, k_ref, v_ref, g_ref, o_ref)

    def fetch(c, p):
        rows = pl.ds(pl.multiple_of(p * 2 * DIM, 16), 2 * DIM)
        return pltpu.make_async_copy(refs[c].at[rows, :], held.at[c, p], in_sem.at[c, p])

    def send(p):
        rows = pl.ds(pl.multiple_of(p * 2 * SEND, 16), 2 * SEND)
        return pltpu.make_async_copy(made.at[p], out_ref.at[:, rows, :], out_sem.at[p])

    for p in range(4):
        for c in range(5):
            fetch(c, p).start()

    row, lane = iota((EXTRA, 128), 0), iota((EXTRA, 128), 1)
    for a in range(8):
        at = row - 24 * a
        mine = (at >= 0) & (at < 24)
        cols = slice(128 * a, 128 * a + 128)
        dot_pick[:, cols] = ones_where(mine & (lane == 112 + at // 4))
        for i, c in enumerate((2, 3)):
            picks[i, :, cols] = ones_where(mine & (lane == at + 24 * c))
    token, lane = iota((128, 256), 0), iota((128, 256), 1)
    pick = (token // 64 == lane // 128) & ((token % 64) // 4 == lane % 128 - 96)
    pick = ones_where(pick)
    lane = iota((2 * DIM, 128), 1)
    body_lane = iota((2, 7, 8, 128), 3) < 96
    shape = (2, 8, TOKENS)
    same = iota(shape, 2) % 4 == iota(shape, 1) % 4

    def head_pair(p, carry):
        for c in range(5):
            fetch(c, p).wait()
        full = [held[c, p].astype(F32) for c in range(4)]
        dots = jnp.sum((full[3] * held[4, p].astype(F32)).reshape(2, DIM, TOKENS), axis=1)
        kept = jnp.where(same, dots[:, None, :], 0.0).reshape(16, TOKENS).astype(BF16)
        stacked = jnp.concatenate([kept[:, 128 * b : 128 * b + 128] for b in range(4)], axis=0)
        tail = dot(stacked, pick, NN)
        tail_more = dot(kept[:, BULK:], dot_pick[...], NN)
        spread = None
        for i, c in enumerate((2, 3)):
            part = dot(held[c, p, :, BULK:], picks[i], NN)
            spread = part if spread is None else spread + part
        fourth = [x[:, BULK : BULK + 128] for x in full]
        blank = jnp.zeros((2 * DIM, 64), F32)
        fifth = [jnp.concatenate([x[:, BULK + 128 :], blank], axis=1) for x in full]
        across = [jnp.where(lane < 16, x, y) for x, y in zip(fifth, fourth)]

        def gather(a):
            b, odd = a // 2, a % 2
            cols = slice(128 * b, 128 * b + 128)
            q, k, v, g = [x[:, cols] for x in full]
            pairs = []
            for x, y in ((q, k), (v, g)):
                if odd:
                    joined = jnp.where(lane < 64, roll(x, 64), y)
                else:
                    joined = jnp.where(lane < 64, x, roll(y, 64))
                pairs.append(joined.reshape(2, TILE, 8, 128))
            source = fourth if a < 5 else across if a == 5 else fifth
            rest = spread[:, 128 * a : 128 * a + 128]
            for c in range(4):
                if c not in (2, 3):
                    at = lane - 24 * c
                    rest = jnp.where((at >= 0) & (at < 24), turn(source[c], 24 * c - 24 * a), rest)
            return pairs, rest.reshape(2, TILE, 8, 128)

        def fold(a, pairs, rest):
            b, odd = a // 2, a % 2
            filler = [turn(rest[:, t], 96 - 32 * n) for t in (7, 8) for n in range(3)]
            here = tail[16 * b : 16 * b + 16, 128 * odd : 128 * odd + 128]
            here = here + tail_more[:, 128 * a : 128 * a + 128]
            filler.append(here.reshape(2, 8, 128))
            return pairs, rest[:, :7], jnp.stack(filler, axis=1)

        def store(a, pairs, rest, filler):
            rest = jnp.where(body_lane, rest, filler)
            message = jnp.concatenate([*pairs, rest], axis=1).reshape(2 * SEND, 128)
            made[p, a] = message.astype(BF16)

        first, second = {}, {}
        for t in range(10):
            if t % 2 == 0 and t < 8:
                first[t], first[t + 1] = gather(t), gather(t + 1)
            if 1 <= t < 9:
                second[t - 1] = fold(t - 1, *first.pop(t - 1))
            if t >= 2:
                store(t - 2, *second.pop(t - 2))
        send(p).start()
        return carry

    lax.fori_loop(0, 4, head_pair, 0)
    for p in range(4):
        send(p).wait()


def unpack_kernel(in_ref, dq_ref, dk_ref, dv_ref, made, sem):
    out_refs = (dq_ref, dk_ref, dv_ref)
    left = iota((2, TILE, 8, 128), 3) < 64
    lane = iota((2 * DIM, 128), 1)
    row = iota((64, 256), 0)
    end_pick = ones_where(iota((64, 256), 1) == 24 * (row // 8) + 16 + row % 8)

    def send(c, p):
        rows = pl.ds(pl.multiple_of(p * 2 * DIM, 16), 2 * DIM)
        return pltpu.make_async_copy(made.at[c, p], out_refs[c].at[rows, :], sem.at[c, p])

    def head_pair(p, carry):
        seconds, ends = [], []

        def gather(b):
            one, two = [
                in_ref[a, pl.ds(pl.multiple_of(p * 2 * BACK, 16), 2 * BACK), :].astype(F32).reshape(2, BACK // 8, 8, 128) for a in (2 * b, 2 * b + 1)
            ]
            first, second = one[:, :TILE], two[:, :TILE]
            third, fourth = one[:, TILE : 2 * TILE], two[:, TILE : 2 * TILE]
            seconds.extend([third.reshape(2 * DIM, 128), fourth.reshape(2 * DIM, 128)])
            ends.extend([one[:, 2 * TILE], two[:, 2 * TILE]])
            return (
                jnp.where(left, first, roll(second, 64)),
                jnp.where(left, roll(first, 64), second),
                jnp.where(left, third, roll(fourth, 64)),
            )

        def store(b, grads):
            for c, grad in enumerate(grads):
                made[c, p, :, 128 * b : 128 * b + 128] = grad.reshape(2 * DIM, 128).astype(BF16)

        def shift(c):
            return [turn(x, 24 * a - 64 - 24 * c) for a, x in enumerate(seconds)]

        def join(c, moved):
            for tile, owners in ((0, range(6)), (1, range(5, 8))):
                total = last[:, 128 * tile : 128 * tile + 128]
                for a in owners:
                    at = lane - (24 * a - 128 * tile)
                    mine = (at >= 0) & (at < (24, 24, 16)[c])
                    total = jnp.where(mine, moved[a], total)
                start = BULK + 128 * tile
                part = total[:, : 128 - 64 * tile].astype(BF16)
                made[c, p, :, start : start + 128 - 64 * tile] = part

        ready = gather(0)
        for b in range(4):
            following = gather(b + 1) if b < 3 else None
            store(b, ready)
            ready = following
        ends = jnp.stack(ends, axis=1).reshape(2, 64, 128).astype(BF16)
        last = [dot(ends[h], end_pick, TN)[:DIM] for h in range(2)]
        last = jnp.concatenate(last, axis=0)
        ready = shift(0)
        for c in range(3):
            following = shift(c + 1) if c < 2 else None
            join(c, ready)
            ready = following
        for c in range(3):
            send(c, p).start()
        return carry

    lax.fori_loop(0, 4, head_pair, 0)
    for p in range(4):
        for c in range(3):
            send(c, p).wait()


def softmax_t(scores):
    top = jnp.max(scores, axis=0, keepdims=True)
    weights = jnp.exp2((scores - top) * EXP_SCALE)
    return weights * (1.0 / jnp.sum(weights, axis=0, keepdims=True))


def time_kernel(in_ref, out_ref, came, held, tails, grads, made, in_sem, out_sem):
    def fetch(part):
        rows = pl.ds(part * FRAMES * SEND // 4, FRAMES * SEND // 4)
        return pltpu.make_async_copy(in_ref.at[rows, :], came.at[rows, :], in_sem.at[part])

    for part in range(4):
        fetch(part).start()

    row = iota((256, 256), 0)
    order = ones_where(iota((256, 256), 1) == 128 * ((row // 4) % 2) + 4 * (row // 8) + row % 4)
    unit = ones_where(iota((DIM, DIM), 0) == iota((DIM, DIM), 1))
    lane = iota((8, 128), 1)
    upper = iota((8, 128), 0) < 4

    def arriving(j):
        firsts, rests, last = [], [], []
        for p in range(2):
            start = pl.multiple_of((2 * j + p) * 2 * SEND, 16)
            x = came[pl.ds(start, 2 * SEND), :].astype(F32).reshape(2, SEND // 8, 8, 128)
            sides, more = [], []
            for f in range(2):
                sides.append(jnp.concatenate([x[f, :16], x[f, TILE:]], axis=0).reshape(256, 128))
                m = x[f, 2 * TILE :]
                ends = [
                    jnp.where(
                        lane < 32,
                        roll(m[t], 32),
                        jnp.where(lane < 64, roll(m[t + 1], 64), roll(m[t + 2], 96)),
                    )
                    for t in (0, 3)
                ]
                more.append(jnp.concatenate([m, ends[0][None], ends[1][None], m], axis=0))
            wide = jnp.concatenate(sides, axis=1).astype(BF16)
            firsts.append(dot(order, wide, NT))
            rests.append(jnp.concatenate([y.reshape(128, 128) for y in more], axis=1))
            last.append(jnp.where(upper, x[0, SEND // 8 - 1], x[1, SEND // 8 - 1]))
        rest = jnp.concatenate(rests, axis=0).astype(BF16)
        return firsts, dot(order[: 8 * 4 * 6], rest, NT), last

    def keep(j, firsts, rest, last):
        for p in range(2):
            at = pl.ds(pl.multiple_of((2 * j + p) * 8, 8), 8)
            for c in range(4):
                start = 128 * (c // 2)
                half = firsts[p][128 * (c % 2) : 128 * (c % 2) + 128, start : start + DIM]
                held[c, 0:16, at, 0:DIM] = half.reshape(16, 8, DIM)
                half = rest[48 * c : 48 * c + 48, 128 * p : 128 * p + DIM]
                held[c, 16:UNITS, at, 0:DIM] = half.reshape(6, 8, DIM)
            tails[at, :] = last[p]

    for part in range(4):
        fetch(part).wait()
        ahead(part, FRAMES // 16, 4, arriving, keep)
    pick = ones_where(iota((32, 128), 1) == iota((32, 128), 0) + 96)
    dots = dot(pick, tails[...].astype(BF16), NT)
    same = iota((ROWS, ROWS), 0) % 4 == iota((ROWS, ROWS), 1) % 4

    def load(u):
        q, k, v, g = [held[c, u, :, 0:DIM].astype(BF16) for c in range(4)]
        return q, k, g, dot(k, q, NT), dot(v, g, NT)

    def middle(u, q, k, g, scores, grad_attend):
        attend = softmax_t(jnp.where(same, scores, -1e30))
        dscore = (attend * (grad_attend - dots[u : u + 1, :])).astype(BF16)
        return q, k, g, attend.astype(BF16), dscore

    def finish(u, q, k, g, attend, dscore):
        grads[0, u, :, 0:DIM] = dot(dscore, k, TN) * SCALE
        grads[1, u, :, 0:DIM] = dot(dscore, q, NN) * SCALE
        grads[2, u, :, 0:DIM] = dot(attend, g, NN)

    loaded, ready = load(0), None
    for u in range(UNITS + 1):
        following = load(u + 1) if u + 1 < UNITS else None
        if u > 0:
            finish(u - 1, *ready)
        if u < UNITS:
            ready = middle(u, *loaded)
        loaded = following

    def swap(x):
        pairs = x.reshape(x.shape[0] // 2, 2, 8, 128)
        even, odd = pairs[:, 0], pairs[:, 1]
        first = jnp.where(upper, even, pltpu.roll(odd, 4, 1))
        second = jnp.where(upper, pltpu.roll(even, 4, 1), odd)
        return first, second

    def leaving(i):
        at = pl.ds(pl.multiple_of(i * 8, 8), 8)
        sets = (
            (grads[0, 0:16, at, :], grads[1, 0:16, at, :]),
            (
                grads[2, 0:16, at, :],
                grads[0, 16:UNITS, at, :],
                grads[1, 16:UNITS, at, :],
                grads[2, 16:20, at, :],
            ),
        )
        turned = []
        for parts in sets:
            rows = jnp.concatenate(swap(jnp.concatenate(parts, axis=0)), axis=0)
            rows = rows.reshape(256, 128)[:, :DIM].astype(BF16)
            turned.append(dot(unit, rows, NT))
        ends = swap(jnp.where(lane < DIM, grads[2, 20:22, at, :], 0.0))
        return turned, ends

    def place(i, turned, ends):
        pieces = []
        for f in range(2):
            pieces += [t[:, 128 * f : 128 * f + 128] for t in turned] + [ends[f][0]]
        start = pl.multiple_of(i * 2 * BACK, 16)
        made[pl.ds(start, 2 * BACK), :] = jnp.concatenate(pieces, axis=0).astype(BF16)

    def send(part):
        rows = pl.ds(part * FRAMES * BACK // 4, FRAMES * BACK // 4)
        return pltpu.make_async_copy(made.at[rows, :], out_ref.at[rows, :], out_sem.at[part])

    for part in range(4):
        ahead(part, FRAMES // 8, 8, leaving, place)
        send(part).start()
    for part in range(4):
        send(part).wait()


def ahead(part, count, block, make, use):
    def step(j, carry):
        base = part * count + j * block
        ready = make(base)
        for t in range(block):
            following = make(base + t + 1) if t + 1 < block else None
            use(base + t, *ready)
            ready = following
        return carry

    lax.fori_loop(0, count // block, step, 0)


def space_kernel(q_ref, k_ref, v_ref, o_ref, g_ref, dq_ref, dk_ref, dv_ref):
    q2, k2, v2, o2, g2 = [ref[...].astype(F32) for ref in (q_ref, k_ref, v_ref, o_ref, g_ref)]
    dots = jnp.sum((g2 * o2).reshape(2, DIM, TOKENS), axis=1)
    grads = ([], [], [])
    for h in range(2):
        part = slice(h * DIM, (h + 1) * DIM)
        q, k, v, g = [x[part].astype(BF16) for x in (q2, k2, v2, g2)]
        k_rows, v_rows = k2[part].T.astype(BF16), v2[part].T.astype(BF16)
        dq, dk, dv = [], None, None
        for start, size in ((0, 256), (256, 256), (512, 192)):
            cols = slice(start, start + size)
            attend = softmax_t(dot(k_rows, q[:, cols], NN))
            shifted = dot(v_rows, g[:, cols], NN) - dots[h : h + 1, cols]
            dscore = (attend * shifted).astype(BF16)
            dq.append(dot(k, dscore, NN))
            dk_part = dot(q[:, cols], dscore, NT)
            dv_part = dot(g[:, cols], attend.astype(BF16), NT)
            dk = dk_part if dk is None else dk + dk_part
            dv = dv_part if dv is None else dv + dv_part
        grads[0].append(jnp.concatenate(dq, axis=1) * SCALE)
        grads[1].append(dk * SCALE)
        grads[2].append(dv)
    for ref, halves in zip((dq_ref, dk_ref, dv_ref), grads):
        ref[...] = jnp.concatenate(halves, axis=0).astype(BF16)


def call(kernel, out_shapes, args, flops, vmem, **specs):
    moved = sum(a.size * 2 for a in args) + sum(math.prod(o) * 2 for o in out_shapes)
    return pl.pallas_call(
        kernel,
        out_shape=tuple(jax.ShapeDtypeStruct(o, BF16) for o in out_shapes),
        compiler_params=pltpu.CompilerParams(vmem_limit_bytes=vmem * 1024 * 1024),
        cost_estimate=pl.CostEstimate(flops=flops, bytes_accessed=moved, transcendentals=0),
        name=kernel.__name__,
        **specs,
    )(*args)


HEAD_PAIR = pl.BlockSpec((2 * DIM, TOKENS), lambda p: (p, 0))


def pack(q, k, v, g, o):
    (sent,) = call(
        pack_kernel,
        [(8, HEADS * SEND, 128)],
        (q, k, v, g, o),
        10**9,
        60,
        in_specs=[pl.BlockSpec(memory_space=pltpu.HBM)] * 5,
        out_specs=(pl.BlockSpec(memory_space=pltpu.HBM),),
        scratch_shapes=[
            pltpu.VMEM((5, 4, 2 * DIM, TOKENS), BF16),
            pltpu.VMEM((4, 8, 2 * SEND, 128), BF16),
            pltpu.VMEM((2, EXTRA, 1024), BF16),
            pltpu.VMEM((EXTRA, 1024), BF16),
            pltpu.SemaphoreType.DMA((5, 4)),
            pltpu.SemaphoreType.DMA((4,)),
        ],
    )
    return sent


def unpack(back):
    return call(
        unpack_kernel,
        [(WIDTH, TOKENS)] * 3,
        (back.reshape(8, HEADS * BACK, 128),),
        10**9,
        50,
        in_specs=[pl.BlockSpec(memory_space=pltpu.VMEM)],
        out_specs=(pl.BlockSpec(memory_space=pltpu.HBM),) * 3,
        scratch_shapes=[
            pltpu.VMEM((3, 4, 2 * DIM, TOKENS), BF16),
            pltpu.SemaphoreType.DMA((3, 4)),
        ],
    )


def time_grads(got):
    return call(
        time_kernel,
        [(FRAMES * BACK, 128)],
        (got,),
        10**10,
        60,
        in_specs=[pl.BlockSpec(memory_space=pltpu.HBM)],
        out_specs=(pl.BlockSpec(memory_space=pltpu.HBM),),
        scratch_shapes=[
            pltpu.VMEM((FRAMES * SEND, 128), BF16),
            pltpu.VMEM((4, UNITS, ROWS, 128), F32),
            pltpu.VMEM((ROWS, 128), F32),
            pltpu.VMEM((3, UNITS, ROWS, 128), F32),
            pltpu.VMEM((FRAMES * BACK, 128), BF16),
            pltpu.SemaphoreType.DMA((4,)),
            pltpu.SemaphoreType.DMA((4,)),
        ],
    )[0]


def space_grads(*args):
    return call(
        space_kernel,
        [(WIDTH, TOKENS)] * 3,
        args,
        4 * 10**10,
        60,
        grid=(4,),
        in_specs=[HEAD_PAIR] * 5,
        out_specs=(HEAD_PAIR,) * 3,
    )


def exchange(x, rows):
    x = x.reshape(FRAMES, rows, 128)
    x = lax.all_to_all(x, "seq", split_axis=0, concat_axis=0, tiled=True)
    return x.reshape(FRAMES * rows, 128)


def body(*args):
    sq, sk, sv, so, sg, tq, tk, tv, to, tg = [jnp.swapaxes(x[0], 0, 1) for x in args]
    got = exchange(pack(tq, tk, tv, tg, to), SEND)
    space = space_grads(sq, sk, sv, so, sg)
    time = unpack(exchange(time_grads(got), BACK))
    return tuple(jnp.swapaxes(x, 0, 1)[None] for x in (*space, *time))


def solution(mesh):
    spec = P(("dp", "seq"), None, None)
    return jax.shard_map(
        body, mesh=mesh, in_specs=(spec,) * 10, out_specs=(spec,) * 6, check_vma=False
    )
```

```python
import math

import jax
import jax.numpy as jnp
from jax import lax
from jax.experimental import pallas as pl
from jax.experimental.pallas import tpu as pltpu
from jax.sharding import PartitionSpec as P

HEADS = 8
DIM = 72
WIDTH = HEADS * DIM
TOKENS = 704
FRAMES = 64
BULK = 512
EXTRA = TOKENS - BULK
SEND = 200
BACK = 152
UNITS = 22
ROWS = 4 * FRAMES
TILE = DIM // 8
SCALE = 1.0 / math.sqrt(DIM)
EXP_SCALE = SCALE * math.log2(math.e)
BF16 = jnp.bfloat16
F32 = jnp.float32
NN = ((1,), (0,))
NT = ((1,), (1,))
TN = ((0,), (0,))


def dot(a, b, dims):
    return lax.dot_general(a, b, (dims, ((), ())), preferred_element_type=F32)


def iota(shape, axis):
    return lax.broadcasted_iota(jnp.int32, shape, axis)


def ones_where(condition):
    return jnp.where(condition, 1.0, 0.0).astype(BF16)


def roll(x, shift):
    return pltpu.roll(x, shift, x.ndim - 1)


def turn(x, shift):
    return roll(x, shift % 128) if shift % 128 else x


def pack_kernel(q_ref, k_ref, v_ref, g_ref, o_ref, out_ref, held, made, picks, dot_pick, in_sem, out_sem):
    refs = (q_ref, k_ref, v_ref, g_ref, o_ref)

    def fetch(c, p):
        rows = pl.ds(pl.multiple_of(p * 2 * DIM, 16), 2 * DIM)
        return pltpu.make_async_copy(refs[c].at[rows, :], held.at[c, p], in_sem.at[c, p])

    def send(p):
        rows = pl.ds(pl.multiple_of(p * 2 * SEND, 16), 2 * SEND)
        return pltpu.make_async_copy(made.at[p], out_ref.at[:, rows, :], out_sem.at[p])

    for p in range(4):
        for c in range(5):
            fetch(c, p).start()

    row, lane = iota((EXTRA, 128), 0), iota((EXTRA, 128), 1)
    for a in range(8):
        at = row - 24 * a
        mine = (at >= 0) & (at < 24)
        cols = slice(128 * a, 128 * a + 128)
        dot_pick[:, cols] = ones_where(mine & (lane == 112 + at // 4))
        for i, c in enumerate((2, 3)):
            picks[i, :, cols] = ones_where(mine & (lane == at + 24 * c))
    token, lane = iota((128, 256), 0), iota((128, 256), 1)
    pick = (token // 64 == lane // 128) & ((token % 64) // 4 == lane % 128 - 96)
    pick = ones_where(pick)
    lane = iota((2 * DIM, 128), 1)
    body_lane = iota((2, 7, 8, 128), 3) < 96
    shape = (2, 8, TOKENS)
    same = iota(shape, 2) % 4 == iota(shape, 1) % 4

    def head_pair(p, carry):
        for c in range(5):
            fetch(c, p).wait()
        full = [held[c, p].astype(F32) for c in range(4)]
        dots = jnp.sum((full[3] * held[4, p].astype(F32)).reshape(2, DIM, TOKENS), axis=1)
        kept = jnp.where(same, dots[:, None, :], 0.0).reshape(16, TOKENS).astype(BF16)
        stacked = jnp.concatenate([kept[:, 128 * b : 128 * b + 128] for b in range(4)], axis=0)
        tail = dot(stacked, pick, NN)
        tail_more = dot(kept[:, BULK:], dot_pick[...], NN)
        spread = None
        for i, c in enumerate((2, 3)):
            part = dot(held[c, p, :, BULK:], picks[i], NN)
            spread = part if spread is None else spread + part
        fourth = [x[:, BULK : BULK + 128] for x in full]
        blank = jnp.zeros((2 * DIM, 64), F32)
        fifth = [jnp.concatenate([x[:, BULK + 128 :], blank], axis=1) for x in full]
        across = [jnp.where(lane < 16, x, y) for x, y in zip(fifth, fourth)]

        def gather(a):
            b, odd = a // 2, a % 2
            cols = slice(128 * b, 128 * b + 128)
            q, k, v, g = [x[:, cols] for x in full]
            pairs = []
            for x, y in ((q, k), (v, g)):
                if odd:
                    joined = jnp.where(lane < 64, roll(x, 64), y)
                else:
                    joined = jnp.where(lane < 64, x, roll(y, 64))
                pairs.append(joined.reshape(2, TILE, 8, 128))
            source = fourth if a < 5 else across if a == 5 else fifth
            rest = spread[:, 128 * a : 128 * a + 128]
            for c in range(4):
                if c not in (2, 3):
                    at = lane - 24 * c
                    rest = jnp.where((at >= 0) & (at < 24), turn(source[c], 24 * c - 24 * a), rest)
            return pairs, rest.reshape(2, TILE, 8, 128)

        def fold(a, pairs, rest):
            b, odd = a // 2, a % 2
            filler = [turn(rest[:, t], 96 - 32 * n) for t in (7, 8) for n in range(3)]
            here = tail[16 * b : 16 * b + 16, 128 * odd : 128 * odd + 128]
            here = here + tail_more[:, 128 * a : 128 * a + 128]
            filler.append(here.reshape(2, 8, 128))
            return pairs, rest[:, :7], jnp.stack(filler, axis=1)

        def store(a, pairs, rest, filler):
            rest = jnp.where(body_lane, rest, filler)
            message = jnp.concatenate([*pairs, rest], axis=1).reshape(2 * SEND, 128)
            made[p, a] = message.astype(BF16)

        first, second = {}, {}
        for t in range(10):
            if t % 2 == 0 and t < 8:
                first[t], first[t + 1] = gather(t), gather(t + 1)
            if 1 <= t < 9:
                second[t - 1] = fold(t - 1, *first.pop(t - 1))
            if t >= 2:
                store(t - 2, *second.pop(t - 2))
        send(p).start()
        return carry

    lax.fori_loop(0, 4, head_pair, 0)
    for p in range(4):
        send(p).wait()


def unpack_kernel(in_ref, dq_ref, dk_ref, dv_ref, made, sem):
    out_refs = (dq_ref, dk_ref, dv_ref)
    left = iota((2, TILE, 8, 128), 3) < 64
    lane = iota((2 * DIM, 128), 1)
    row = iota((64, 256), 0)
    end_pick = ones_where(iota((64, 256), 1) == 24 * (row // 8) + 16 + row % 8)

    def send(c, p):
        rows = pl.ds(pl.multiple_of(p * 2 * DIM, 16), 2 * DIM)
        return pltpu.make_async_copy(made.at[c, p], out_refs[c].at[rows, :], sem.at[c, p])

    def head_pair(p, carry):
        seconds, ends = [], []

        def gather(b):
            one, two = [
                in_ref[a, pl.ds(pl.multiple_of(p * 2 * BACK, 16), 2 * BACK), :].astype(F32).reshape(2, BACK // 8, 8, 128) for a in (2 * b, 2 * b + 1)
            ]
            first, second = one[:, :TILE], two[:, :TILE]
            third, fourth = one[:, TILE : 2 * TILE], two[:, TILE : 2 * TILE]
            seconds.extend([third.reshape(2 * DIM, 128), fourth.reshape(2 * DIM, 128)])
            ends.extend([one[:, 2 * TILE], two[:, 2 * TILE]])
            mixed = roll(jnp.where(left, second, first), 64)
            return (
                jnp.where(left, first, mixed),
                jnp.where(left, mixed, second),
                jnp.where(left, third, roll(fourth, 64)),
            )

        def store(b, grads):
            for c, grad in enumerate(grads):
                made[c, p, :, 128 * b : 128 * b + 128] = grad.reshape(2 * DIM, 128).astype(BF16)

        def shift(c):
            return [turn(x, 24 * a - 64 - 24 * c) for a, x in enumerate(seconds)]

        def join(c, moved):
            for tile, owners in ((0, range(6)), (1, range(5, 8))):
                total = last[:, 128 * tile : 128 * tile + 128]
                for a in owners:
                    at = lane - (24 * a - 128 * tile)
                    mine = (at >= 0) & (at < (24, 24, 16)[c])
                    total = jnp.where(mine, moved[a], total)
                start = BULK + 128 * tile
                part = total[:, : 128 - 64 * tile].astype(BF16)
                made[c, p, :, start : start + 128 - 64 * tile] = part

        ready = gather(0)
        for b in range(4):
            following = gather(b + 1) if b < 3 else None
            if b == 3:
                moved = shift(0)
            store(b, ready)
            ready = following
        ends = jnp.stack(ends, axis=1).reshape(2, 64, 128).astype(BF16)
        last = [dot(ends[h], end_pick, TN)[:DIM] for h in range(2)]
        last = jnp.concatenate(last, axis=0)
        for c in range(3):
            following = shift(c + 1) if c < 2 else None
            join(c, moved)
            send(c, p).start()
            moved = following
        return carry

    lax.fori_loop(0, 4, head_pair, 0, unroll=True)
    for p in range(4):
        for c in range(3):
            send(c, p).wait()


def softmax_t(scores):
    top = jnp.max(scores, axis=0, keepdims=True)
    weights = jnp.exp2((scores - top) * EXP_SCALE)
    return weights * (1.0 / jnp.sum(weights, axis=0, keepdims=True))


def time_kernel(in_ref, out_ref, came, held, tails, grads, made, in_sem, out_sem):
    def fetch(part):
        rows = pl.ds(part * FRAMES * SEND // 4, FRAMES * SEND // 4)
        return pltpu.make_async_copy(in_ref.at[rows, :], came.at[rows, :], in_sem.at[part])

    for part in range(4):
        fetch(part).start()

    row = iota((256, 256), 0)
    order = ones_where(iota((256, 256), 1) == 128 * ((row // 4) % 2) + 4 * (row // 8) + row % 4)
    unit = ones_where(iota((DIM, DIM), 0) == iota((DIM, DIM), 1))
    lane = iota((8, 128), 1)
    upper = iota((8, 128), 0) < 4

    def arriving(j):
        firsts, rests, last = [], [], []
        for p in range(2):
            start = pl.multiple_of((2 * j + p) * 2 * SEND, 16)
            x = came[pl.ds(start, 2 * SEND), :].astype(F32).reshape(2, SEND // 8, 8, 128)
            sides, more = [], []
            for f in range(2):
                sides.append(jnp.concatenate([x[f, :16], x[f, TILE:]], axis=0).reshape(256, 128))
                m = x[f, 2 * TILE :]
                ends = [
                    jnp.where(
                        lane < 32,
                        roll(m[t], 32),
                        jnp.where(lane < 64, roll(m[t + 1], 64), roll(m[t + 2], 96)),
                    )
                    for t in (0, 3)
                ]
                more.append(jnp.concatenate([m, ends[0][None], ends[1][None], m], axis=0))
            wide = jnp.concatenate(sides, axis=1).astype(BF16)
            firsts.append(wide)
            rests.append(jnp.concatenate([y.reshape(128, 128) for y in more], axis=1))
            last.append(jnp.where(upper, x[0, SEND // 8 - 1], x[1, SEND // 8 - 1]))
        rest = jnp.concatenate(rests, axis=0).astype(BF16)
        return firsts, rest, last

    def ordering(j, firsts, rest, last):
        return [dot(order, x, NT) for x in firsts], dot(order[: 8 * 4 * 6], rest, NT), last

    def keep(j, firsts, rest, last):
        at = pl.ds(pl.multiple_of(j * 16, 16), 16)
        for c in range(4):
            start = 128 * (c // 2)
            rows = slice(128 * (c % 2), 128 * (c % 2) + 128)
            halves = [x[rows, start : start + DIM].reshape(16, 8, DIM) for x in firsts]
            held[c, 0:16, at, 0:DIM] = jnp.concatenate(halves, axis=1).astype(BF16)
            rows = slice(48 * c, 48 * c + 48)
            halves = [rest[rows, x : x + DIM].reshape(6, 8, DIM) for x in (0, 128)]
            held[c, 16:UNITS, at, 0:DIM] = jnp.concatenate(halves, axis=1).astype(BF16)
        tails[at, :] = jnp.concatenate(last, axis=0)

    for part in range(4):
        fetch(part).wait()
        ahead(part, FRAMES // 16, 4, arriving, ordering, keep)
    pick = ones_where(iota((32, 128), 1) == iota((32, 128), 0) + 96)
    dots = dot(pick, tails[...].astype(BF16), NT)
    same = iota((ROWS, ROWS), 0) % 4 == iota((ROWS, ROWS), 1) % 4

    def load(u):
        q, k, v, g = [held[c, u, :, 0:DIM] for c in range(4)]
        return q, k, g, dot(k, q, NT), dot(v, g, NT)

    def middle(u, q, k, g, scores, grad_attend):
        attend = softmax_t(jnp.where(same, scores, -1e30))
        dscore = (attend * (grad_attend - dots[u : u + 1, :])).astype(BF16)
        return q, k, g, attend.astype(BF16), dscore

    def finish(u, q, k, g, attend, dscore):
        grads[0, u, :, 0:DIM] = dot(dscore, k, TN) * SCALE
        grads[1, u, :, 0:DIM] = dot(dscore, q, NN) * SCALE
        grads[2, u, :, 0:DIM] = dot(attend, g, NN)

    loaded, ready = load(0), None
    for u in range(UNITS + 1):
        following = load(u + 1) if u + 1 < UNITS else None
        if u > 0:
            finish(u - 1, *ready)
        if u < UNITS:
            ready = middle(u, *loaded)
        loaded = following

    def swap(x):
        pairs = x.reshape(x.shape[0] // 2, 2, 8, 128)
        even, odd = pairs[:, 0], pairs[:, 1]
        first = jnp.where(upper, even, pltpu.roll(odd, 4, 1))
        second = jnp.where(upper, pltpu.roll(even, 4, 1), odd)
        return first, second

    def leaving(i):
        at = pl.ds(pl.multiple_of(i * 8, 8), 8)
        sets = (
            (grads[0, 0:16, at, :], grads[1, 0:16, at, :]),
            (
                grads[2, 0:16, at, :],
                grads[0, 16:UNITS, at, :],
                grads[1, 16:UNITS, at, :],
                grads[2, 16:20, at, :],
            ),
        )
        turned = []
        for parts in sets:
            rows = jnp.concatenate(swap(jnp.concatenate(parts, axis=0)), axis=0)
            turned.append(rows.reshape(256, 128)[:, :DIM].astype(BF16))
        ends = swap(jnp.where(lane < DIM, grads[2, 20:22, at, :], 0.0))
        return turned, ends

    def turning(i, rows, ends):
        return [dot(unit, x, NT) for x in rows], ends

    def place(i, turned, ends):
        pieces = []
        for f in range(2):
            pieces += [t[:, 128 * f : 128 * f + 128] for t in turned] + [ends[f][0]]
        start = pl.multiple_of(i * 2 * BACK, 16)
        made[pl.ds(start, 2 * BACK), :] = jnp.concatenate(pieces, axis=0).astype(BF16)

    def send(part):
        rows = pl.ds(part * FRAMES * BACK // 4, FRAMES * BACK // 4)
        return pltpu.make_async_copy(made.at[rows, :], out_ref.at[rows, :], out_sem.at[part])

    for part in range(4):
        ahead(part, FRAMES // 8, 8, leaving, turning, place)
        send(part).start()
    for part in range(4):
        send(part).wait()


def ahead(part, count, block, make, work, use):
    def step(j, carry):
        base = part * count + j * block
        made, worked = {}, {}
        for t in range(block + 2):
            if t < block:
                made[t] = make(base + t)
            if 1 <= t <= block:
                worked[t - 1] = work(base + t - 1, *made.pop(t - 1))
            if t >= 2:
                use(base + t - 2, *worked.pop(t - 2))
        return carry

    lax.fori_loop(0, count // block, step, 0)


def space_kernel(q_ref, k_ref, v_ref, o_ref, g_ref, dq_ref, dk_ref, dv_ref):
    q2, k2, v2, o2, g2 = [ref[...].astype(F32) for ref in (q_ref, k_ref, v_ref, o_ref, g_ref)]
    dots = jnp.sum((g2 * o2).reshape(2, DIM, TOKENS), axis=1)
    grads = ([], [], [])
    for h in range(2):
        part = slice(h * DIM, (h + 1) * DIM)
        q, k, v, g = [x[part].astype(BF16) for x in (q2, k2, v2, g2)]
        k_rows, v_rows = k2[part].T.astype(BF16), v2[part].T.astype(BF16)
        dq, dk, dv = [], None, None
        for start, size in ((0, 256), (256, 256), (512, 192)):
            cols = slice(start, start + size)
            attend = softmax_t(dot(k_rows, q[:, cols], NN))
            shifted = dot(v_rows, g[:, cols], NN) - dots[h : h + 1, cols]
            dscore = (attend * shifted).astype(BF16)
            dq.append(dot(k, dscore, NN))
            dk_part = dot(q[:, cols], dscore, NT)
            dv_part = dot(g[:, cols], attend.astype(BF16), NT)
            dk = dk_part if dk is None else dk + dk_part
            dv = dv_part if dv is None else dv + dv_part
        grads[0].append(jnp.concatenate(dq, axis=1) * SCALE)
        grads[1].append(dk * SCALE)
        grads[2].append(dv)
    for ref, halves in zip((dq_ref, dk_ref, dv_ref), grads):
        ref[...] = jnp.concatenate(halves, axis=0).astype(BF16)


def call(kernel, out_shapes, args, flops, vmem, **specs):
    moved = sum(a.size * 2 for a in args) + sum(math.prod(o) * 2 for o in out_shapes)
    return pl.pallas_call(
        kernel,
        out_shape=tuple(jax.ShapeDtypeStruct(o, BF16) for o in out_shapes),
        compiler_params=pltpu.CompilerParams(vmem_limit_bytes=vmem * 1024 * 1024),
        cost_estimate=pl.CostEstimate(flops=flops, bytes_accessed=moved, transcendentals=0),
        name=kernel.__name__,
        **specs,
    )(*args)


HEAD_PAIR = pl.BlockSpec((2 * DIM, TOKENS), lambda p: (p, 0))


def pack(q, k, v, g, o):
    (sent,) = call(
        pack_kernel,
        [(8, HEADS * SEND, 128)],
        (q, k, v, g, o),
        10**9,
        60,
        in_specs=[pl.BlockSpec(memory_space=pltpu.HBM)] * 5,
        out_specs=(pl.BlockSpec(memory_space=pltpu.HBM),),
        scratch_shapes=[
            pltpu.VMEM((5, 4, 2 * DIM, TOKENS), BF16),
            pltpu.VMEM((4, 8, 2 * SEND, 128), BF16),
            pltpu.VMEM((2, EXTRA, 1024), BF16),
            pltpu.VMEM((EXTRA, 1024), BF16),
            pltpu.SemaphoreType.DMA((5, 4)),
            pltpu.SemaphoreType.DMA((4,)),
        ],
    )
    return sent


def unpack(back):
    return call(
        unpack_kernel,
        [(WIDTH, TOKENS)] * 3,
        (back.reshape(8, HEADS * BACK, 128),),
        10**9,
        50,
        in_specs=[pl.BlockSpec(memory_space=pltpu.VMEM)],
        out_specs=(pl.BlockSpec(memory_space=pltpu.HBM),) * 3,
        scratch_shapes=[
            pltpu.VMEM((3, 4, 2 * DIM, TOKENS), BF16),
            pltpu.SemaphoreType.DMA((3, 4)),
        ],
    )


def time_grads(got):
    return call(
        time_kernel,
        [(FRAMES * BACK, 128)],
        (got,),
        10**10,
        60,
        in_specs=[pl.BlockSpec(memory_space=pltpu.HBM)],
        out_specs=(pl.BlockSpec(memory_space=pltpu.HBM),),
        scratch_shapes=[
            pltpu.VMEM((FRAMES * SEND, 128), BF16),
            pltpu.VMEM((4, UNITS, ROWS, 128), BF16),
            pltpu.VMEM((ROWS, 128), F32),
            pltpu.VMEM((3, UNITS, ROWS, 128), F32),
            pltpu.VMEM((FRAMES * BACK, 128), BF16),
            pltpu.SemaphoreType.DMA((4,)),
            pltpu.SemaphoreType.DMA((4,)),
        ],
    )[0]


def space_grads(*args):
    return call(
        space_kernel,
        [(WIDTH, TOKENS)] * 3,
        args,
        4 * 10**10,
        60,
        grid=(4,),
        in_specs=[HEAD_PAIR] * 5,
        out_specs=(HEAD_PAIR,) * 3,
    )


def exchange(x, rows):
    x = x.reshape(FRAMES, rows, 128)
    x = lax.all_to_all(x, "seq", split_axis=0, concat_axis=0, tiled=True)
    return x.reshape(FRAMES * rows, 128)


def body(*args):
    sq, sk, sv, so, sg, tq, tk, tv, to, tg = [jnp.swapaxes(x[0], 0, 1) for x in args]
    got = exchange(pack(tq, tk, tv, tg, to), SEND)
    space = space_grads(sq, sk, sv, so, sg)
    time = unpack(exchange(time_grads(got), BACK))
    return tuple(jnp.swapaxes(x, 0, 1)[None] for x in (*space, *time))


def solution(mesh):
    spec = P(("dp", "seq"), None, None)
    return jax.shard_map(
        body, mesh=mesh, in_specs=(spec,) * 10, out_specs=(spec,) * 6, check_vma=False
    )
```

```python
import math

import jax
import jax.numpy as jnp
from jax import lax
from jax.experimental import pallas as pl
from jax.experimental.pallas import tpu as pltpu
from jax.sharding import Mesh
from jax.sharding import PartitionSpec as P

HEADS = 8
DIM = 72
WIDTH = HEADS * DIM
TOKENS = 704
FRAMES = 64
BULK = 512
EXTRA = TOKENS - BULK
SEND = 200
BACK = 152
UNITS = 22
ROWS = 4 * FRAMES
TILE = DIM // 8
SCALE = 1.0 / math.sqrt(DIM)
EXP_SCALE = SCALE * math.log2(math.e)
PEERS = ("x", "z", "y")
BF16 = jnp.bfloat16
F32 = jnp.float32
NN = ((1,), (0,))
NT = ((1,), (1,))
TN = ((0,), (0,))


def dot(a, b, dims):
    return lax.dot_general(a, b, (dims, ((), ())), preferred_element_type=F32)


def iota(shape, axis):
    return lax.broadcasted_iota(jnp.int32, shape, axis)


def ones_where(condition):
    return jnp.where(condition, 1.0, 0.0).astype(BF16)


def roll(x, shift):
    return pltpu.roll(x, shift, x.ndim - 1)


def turn(x, shift):
    return roll(x, shift % 128) if shift % 128 else x


def pack_kernel(q_ref, k_ref, v_ref, g_ref, o_ref, out_ref, held, made, picks, dot_pick, in_sem, out_sem):
    refs = (q_ref, k_ref, v_ref, g_ref, o_ref)

    def fetch(c, p):
        rows = pl.ds(pl.multiple_of(p * 2 * DIM, 16), 2 * DIM)
        return pltpu.make_async_copy(refs[c].at[rows, :], held.at[c, p], in_sem.at[c, p])

    def send(p):
        rows = pl.ds(pl.multiple_of(p * 2 * SEND, 16), 2 * SEND)
        return pltpu.make_async_copy(made.at[p], out_ref.at[:, rows, :], out_sem.at[p])

    for p in range(4):
        for c in range(5):
            fetch(c, p).start()

    row, lane = iota((EXTRA, 128), 0), iota((EXTRA, 128), 1)
    for a in range(8):
        at = row - 24 * a
        mine = (at >= 0) & (at < 24)
        cols = slice(128 * a, 128 * a + 128)
        dot_pick[:, cols] = ones_where(mine & (lane == 112 + at // 4))
        for i, c in enumerate((2, 3)):
            picks[i, :, cols] = ones_where(mine & (lane == at + 24 * c))
    token, lane = iota((128, 256), 0), iota((128, 256), 1)
    pick = (token // 64 == lane // 128) & ((token % 64) // 4 == lane % 128 - 96)
    pick = ones_where(pick)
    lane = iota((2 * DIM, 128), 1)
    body_lane = iota((2, 7, 8, 128), 3) < 96
    shape = (2, 8, TOKENS)
    same = iota(shape, 2) % 4 == iota(shape, 1) % 4

    def head_pair(p, carry):
        for c in range(5):
            fetch(c, p).wait()
        full = [held[c, p].astype(F32) for c in range(4)]
        dots = jnp.sum((full[3] * held[4, p].astype(F32)).reshape(2, DIM, TOKENS), axis=1)
        kept = jnp.where(same, dots[:, None, :], 0.0).reshape(16, TOKENS).astype(BF16)
        stacked = jnp.concatenate([kept[:, 128 * b : 128 * b + 128] for b in range(4)], axis=0)
        tail = dot(stacked, pick, NN)
        tail_more = dot(kept[:, BULK:], dot_pick[...], NN)
        spread = None
        for i, c in enumerate((2, 3)):
            part = dot(held[c, p, :, BULK:], picks[i], NN)
            spread = part if spread is None else spread + part
        fourth = [x[:, BULK : BULK + 128] for x in full]
        blank = jnp.zeros((2 * DIM, 64), F32)
        fifth = [jnp.concatenate([x[:, BULK + 128 :], blank], axis=1) for x in full]
        across = [jnp.where(lane < 16, x, y) for x, y in zip(fifth, fourth)]

        def gather(a):
            b, odd = a // 2, a % 2
            cols = slice(128 * b, 128 * b + 128)
            q, k, v, g = [x[:, cols] for x in full]
            pairs = []
            for x, y in ((q, k), (v, g)):
                if odd:
                    joined = jnp.where(lane < 64, roll(x, 64), y)
                else:
                    joined = jnp.where(lane < 64, x, roll(y, 64))
                pairs.append(joined.reshape(2, TILE, 8, 128))
            source = fourth if a < 5 else across if a == 5 else fifth
            rest = spread[:, 128 * a : 128 * a + 128]
            for c in range(4):
                if c not in (2, 3):
                    at = lane - 24 * c
                    rest = jnp.where((at >= 0) & (at < 24), turn(source[c], 24 * c - 24 * a), rest)
            return pairs, rest.reshape(2, TILE, 8, 128)

        def fold(a, pairs, rest):
            b, odd = a // 2, a % 2
            filler = [turn(rest[:, t], 96 - 32 * n) for t in (7, 8) for n in range(3)]
            here = tail[16 * b : 16 * b + 16, 128 * odd : 128 * odd + 128]
            here = here + tail_more[:, 128 * a : 128 * a + 128]
            filler.append(here.reshape(2, 8, 128))
            return pairs, rest[:, :7], jnp.stack(filler, axis=1)

        def store(a, pairs, rest, filler):
            rest = jnp.where(body_lane, rest, filler)
            message = jnp.concatenate([*pairs, rest], axis=1).reshape(2 * SEND, 128)
            made[p, a] = message.astype(BF16)

        first, second = {}, {}
        for t in range(10):
            if t % 2 == 0 and t < 8:
                first[t], first[t + 1] = gather(t), gather(t + 1)
            if 1 <= t < 9:
                second[t - 1] = fold(t - 1, *first.pop(t - 1))
            if t >= 2:
                store(t - 2, *second.pop(t - 2))
        send(p).start()
        return carry

    lax.fori_loop(0, 4, head_pair, 0)
    for p in range(4):
        send(p).wait()


def unpack_kernel(in_ref, dq_ref, dk_ref, dv_ref, made, sem):
    out_refs = (dq_ref, dk_ref, dv_ref)
    left = iota((2, TILE, 8, 128), 3) < 64
    lane = iota((2 * DIM, 128), 1)
    row = iota((64, 256), 0)
    end_pick = ones_where(iota((64, 256), 1) == 24 * (row // 8) + 16 + row % 8)

    def send(c, p):
        rows = pl.ds(pl.multiple_of(p * 2 * DIM, 16), 2 * DIM)
        return pltpu.make_async_copy(made.at[c, p], out_refs[c].at[rows, :], sem.at[c, p])

    def head_pair(p, carry):
        seconds, ends = [], []

        def gather(b):
            one, two = [
                in_ref[a, pl.ds(pl.multiple_of(p * 2 * BACK, 16), 2 * BACK), :].astype(F32).reshape(2, BACK // 8, 8, 128) for a in (2 * b, 2 * b + 1)
            ]
            first, second = one[:, :TILE], two[:, :TILE]
            third, fourth = one[:, TILE : 2 * TILE], two[:, TILE : 2 * TILE]
            seconds.extend([third.reshape(2 * DIM, 128), fourth.reshape(2 * DIM, 128)])
            ends.extend([one[:, 2 * TILE], two[:, 2 * TILE]])
            mixed = roll(jnp.where(left, second, first), 64)
            return (
                jnp.where(left, first, mixed),
                jnp.where(left, mixed, second),
                jnp.where(left, third, roll(fourth, 64)),
            )

        def store(b, grads):
            for c, grad in enumerate(grads):
                made[c, p, :, 128 * b : 128 * b + 128] = grad.reshape(2 * DIM, 128).astype(BF16)

        def shift(c):
            return [turn(x, 24 * a - 64 - 24 * c) for a, x in enumerate(seconds)]

        def join(c, moved):
            for tile, owners in ((0, range(6)), (1, range(5, 8))):
                total = last[:, 128 * tile : 128 * tile + 128]
                for a in owners:
                    at = lane - (24 * a - 128 * tile)
                    mine = (at >= 0) & (at < (24, 24, 16)[c])
                    total = jnp.where(mine, moved[a], total)
                start = BULK + 128 * tile
                part = total[:, : 128 - 64 * tile].astype(BF16)
                made[c, p, :, start : start + 128 - 64 * tile] = part

        ready = gather(0)
        for b in range(4):
            following = gather(b + 1) if b < 3 else None
            if b == 3:
                moved = shift(0)
            store(b, ready)
            ready = following
        ends = jnp.stack(ends, axis=1).reshape(2, 64, 128).astype(BF16)
        last = [dot(ends[h], end_pick, TN)[:DIM] for h in range(2)]
        last = jnp.concatenate(last, axis=0)
        for c in range(3):
            following = shift(c + 1) if c < 2 else None
            join(c, moved)
            send(c, p).start()
            moved = following
        return carry

    lax.fori_loop(0, 4, head_pair, 0, unroll=True)
    for p in range(4):
        for c in range(3):
            send(c, p).wait()


def softmax_t(scores):
    top = jnp.max(scores, axis=0, keepdims=True)
    weights = jnp.exp2((scores - top) * EXP_SCALE)
    return weights * (1.0 / jnp.sum(weights, axis=0, keepdims=True))


def time_kernel(in_ref, out_ref, came, held, tails, grads, made, in_sem, out_sem):
    def fetch(part):
        rows = pl.ds(part * FRAMES * SEND // 4, FRAMES * SEND // 4)
        return pltpu.make_async_copy(in_ref.at[rows, :], came.at[rows, :], in_sem.at[part])

    for part in range(4):
        fetch(part).start()

    row = iota((256, 256), 0)
    order = ones_where(iota((256, 256), 1) == 128 * ((row // 4) % 2) + 4 * (row // 8) + row % 4)
    unit = ones_where(iota((DIM, DIM), 0) == iota((DIM, DIM), 1))
    lane = iota((8, 128), 1)
    upper = iota((8, 128), 0) < 4

    def arriving(j):
        firsts, rests, last = [], [], []
        for p in range(2):
            start = pl.multiple_of((2 * j + p) * 2 * SEND, 16)
            x = came[pl.ds(start, 2 * SEND), :].astype(F32).reshape(2, SEND // 8, 8, 128)
            sides, more = [], []
            for f in range(2):
                sides.append(jnp.concatenate([x[f, :16], x[f, TILE:]], axis=0).reshape(256, 128))
                m = x[f, 2 * TILE :]
                ends = [
                    jnp.where(
                        lane < 32,
                        roll(m[t], 32),
                        jnp.where(lane < 64, roll(m[t + 1], 64), roll(m[t + 2], 96)),
                    )
                    for t in (0, 3)
                ]
                more.append(jnp.concatenate([m, ends[0][None], ends[1][None], m], axis=0))
            wide = jnp.concatenate(sides, axis=1).astype(BF16)
            firsts.append(wide)
            rests.append(jnp.concatenate([y.reshape(128, 128) for y in more], axis=1))
            last.append(jnp.where(upper, x[0, SEND // 8 - 1], x[1, SEND // 8 - 1]))
        rest = jnp.concatenate(rests, axis=0).astype(BF16)
        return firsts, rest, last

    def ordering(j, firsts, rest, last):
        return [dot(order, x, NT) for x in firsts], dot(order[: 8 * 4 * 6], rest, NT), last

    def keep(j, firsts, rest, last):
        at = pl.ds(pl.multiple_of(j * 16, 16), 16)
        for c in range(4):
            start = 128 * (c // 2)
            rows = slice(128 * (c % 2), 128 * (c % 2) + 128)
            halves = [x[rows, start : start + DIM].reshape(16, 8, DIM) for x in firsts]
            held[c, 0:16, at, 0:DIM] = jnp.concatenate(halves, axis=1).astype(BF16)
            rows = slice(48 * c, 48 * c + 48)
            halves = [rest[rows, x : x + DIM].reshape(6, 8, DIM) for x in (0, 128)]
            held[c, 16:UNITS, at, 0:DIM] = jnp.concatenate(halves, axis=1).astype(BF16)
        tails[at, :] = jnp.concatenate(last, axis=0)

    for part in range(4):
        fetch(part).wait()
        ahead(part, FRAMES // 16, 4, arriving, ordering, keep)
    pick = ones_where(iota((32, 128), 1) == iota((32, 128), 0) + 96)
    dots = dot(pick, tails[...].astype(BF16), NT)
    same = iota((ROWS, ROWS), 0) % 4 == iota((ROWS, ROWS), 1) % 4

    def load(u):
        q, k, v, g = [held[c, u, :, 0:DIM] for c in range(4)]
        return q, k, g, dot(k, q, NT), dot(v, g, NT)

    def middle(u, q, k, g, scores, grad_attend):
        attend = softmax_t(jnp.where(same, scores, -1e30))
        dscore = (attend * (grad_attend - dots[u : u + 1, :])).astype(BF16)
        return q, k, g, attend.astype(BF16), dscore

    def finish(u, q, k, g, attend, dscore):
        grads[0, u, :, 0:DIM] = dot(dscore, k, TN) * SCALE
        grads[1, u, :, 0:DIM] = dot(dscore, q, NN) * SCALE
        grads[2, u, :, 0:DIM] = dot(attend, g, NN)

    loaded, ready = load(0), None
    for u in range(UNITS + 1):
        following = load(u + 1) if u + 1 < UNITS else None
        if u > 0:
            finish(u - 1, *ready)
        if u < UNITS:
            ready = middle(u, *loaded)
        loaded = following

    def swap(x):
        pairs = x.reshape(x.shape[0] // 2, 2, 8, 128)
        even, odd = pairs[:, 0], pairs[:, 1]
        first = jnp.where(upper, even, pltpu.roll(odd, 4, 1))
        second = jnp.where(upper, pltpu.roll(even, 4, 1), odd)
        return first, second

    def leaving(i):
        at = pl.ds(pl.multiple_of(i * 8, 8), 8)
        sets = (
            (grads[0, 0:16, at, :], grads[1, 0:16, at, :]),
            (
                grads[2, 0:16, at, :],
                grads[0, 16:UNITS, at, :],
                grads[1, 16:UNITS, at, :],
                grads[2, 16:20, at, :],
            ),
        )
        turned = []
        for parts in sets:
            rows = jnp.concatenate(swap(jnp.concatenate(parts, axis=0)), axis=0)
            turned.append(rows.reshape(256, 128)[:, :DIM].astype(BF16))
        ends = swap(jnp.where(lane < DIM, grads[2, 20:22, at, :], 0.0))
        return turned, ends

    def turning(i, rows, ends):
        return [dot(unit, x, NT) for x in rows], ends

    def place(i, turned, ends):
        pieces = []
        for f in range(2):
            pieces += [t[:, 128 * f : 128 * f + 128] for t in turned] + [ends[f][0]]
        start = pl.multiple_of(i * 2 * BACK, 16)
        made[pl.ds(start, 2 * BACK), :] = jnp.concatenate(pieces, axis=0).astype(BF16)

    def send(part):
        rows = pl.ds(part * FRAMES * BACK // 4, FRAMES * BACK // 4)
        return pltpu.make_async_copy(made.at[rows, :], out_ref.at[rows, :], out_sem.at[part])

    for part in range(4):
        ahead(part, FRAMES // 8, 8, leaving, turning, place)
        send(part).start()
    for part in range(4):
        send(part).wait()


def ahead(part, count, block, make, work, use):
    def step(j, carry):
        base = part * count + j * block
        made, worked = {}, {}
        for t in range(block + 2):
            if t < block:
                made[t] = make(base + t)
            if 1 <= t <= block:
                worked[t - 1] = work(base + t - 1, *made.pop(t - 1))
            if t >= 2:
                use(base + t - 2, *worked.pop(t - 2))
        return carry

    lax.fori_loop(0, count // block, step, 0)


def space_kernel(q_ref, k_ref, v_ref, o_ref, g_ref, dq_ref, dk_ref, dv_ref):
    q2, k2, v2, o2, g2 = [ref[...].astype(F32) for ref in (q_ref, k_ref, v_ref, o_ref, g_ref)]
    dots = jnp.sum((g2 * o2).reshape(2, DIM, TOKENS), axis=1)
    grads = ([], [], [])
    for h in range(2):
        part = slice(h * DIM, (h + 1) * DIM)
        q, k, v, g = [x[part].astype(BF16) for x in (q2, k2, v2, g2)]
        k_rows, v_rows = k2[part].T.astype(BF16), v2[part].T.astype(BF16)
        dq, dk, dv = [], None, None
        for start, size in ((0, 256), (256, 256), (512, 192)):
            cols = slice(start, start + size)
            attend = softmax_t(dot(k_rows, q[:, cols], NN))
            shifted = dot(v_rows, g[:, cols], NN) - dots[h : h + 1, cols]
            dscore = (attend * shifted).astype(BF16)
            dq.append(dot(k, dscore, NN))
            dk_part = dot(q[:, cols], dscore, NT)
            dv_part = dot(g[:, cols], attend.astype(BF16), NT)
            dk = dk_part if dk is None else dk + dk_part
            dv = dv_part if dv is None else dv + dv_part
        grads[0].append(jnp.concatenate(dq, axis=1) * SCALE)
        grads[1].append(dk * SCALE)
        grads[2].append(dv)
    for ref, halves in zip((dq_ref, dk_ref, dv_ref), grads):
        ref[...] = jnp.concatenate(halves, axis=0).astype(BF16)


def call(kernel, out_shapes, args, flops, vmem, **specs):
    moved = sum(a.size * 2 for a in args) + sum(math.prod(o) * 2 for o in out_shapes)
    return pl.pallas_call(
        kernel,
        out_shape=tuple(jax.ShapeDtypeStruct(o, BF16) for o in out_shapes),
        compiler_params=pltpu.CompilerParams(vmem_limit_bytes=vmem * 1024 * 1024),
        cost_estimate=pl.CostEstimate(flops=flops, bytes_accessed=moved, transcendentals=0),
        name=kernel.__name__,
        **specs,
    )(*args)


HEAD_PAIR = pl.BlockSpec((2 * DIM, TOKENS), lambda p: (p, 0))


def pack(q, k, v, g, o):
    (sent,) = call(
        pack_kernel,
        [(8, HEADS * SEND, 128)],
        (q, k, v, g, o),
        10**9,
        60,
        in_specs=[pl.BlockSpec(memory_space=pltpu.HBM)] * 5,
        out_specs=(pl.BlockSpec(memory_space=pltpu.HBM),),
        scratch_shapes=[
            pltpu.VMEM((5, 4, 2 * DIM, TOKENS), BF16),
            pltpu.VMEM((4, 8, 2 * SEND, 128), BF16),
            pltpu.VMEM((2, EXTRA, 1024), BF16),
            pltpu.VMEM((EXTRA, 1024), BF16),
            pltpu.SemaphoreType.DMA((5, 4)),
            pltpu.SemaphoreType.DMA((4,)),
        ],
    )
    return sent


def unpack(back):
    return call(
        unpack_kernel,
        [(WIDTH, TOKENS)] * 3,
        (back.reshape(8, HEADS * BACK, 128),),
        10**9,
        50,
        in_specs=[pl.BlockSpec(memory_space=pltpu.VMEM)],
        out_specs=(pl.BlockSpec(memory_space=pltpu.HBM),) * 3,
        scratch_shapes=[
            pltpu.VMEM((3, 4, 2 * DIM, TOKENS), BF16),
            pltpu.SemaphoreType.DMA((3, 4)),
        ],
    )


def time_grads(got):
    return call(
        time_kernel,
        [(FRAMES * BACK, 128)],
        (got,),
        10**10,
        60,
        in_specs=[pl.BlockSpec(memory_space=pltpu.HBM)],
        out_specs=(pl.BlockSpec(memory_space=pltpu.HBM),),
        scratch_shapes=[
            pltpu.VMEM((FRAMES * SEND, 128), BF16),
            pltpu.VMEM((4, UNITS, ROWS, 128), BF16),
            pltpu.VMEM((ROWS, 128), F32),
            pltpu.VMEM((3, UNITS, ROWS, 128), F32),
            pltpu.VMEM((FRAMES * BACK, 128), BF16),
            pltpu.SemaphoreType.DMA((4,)),
            pltpu.SemaphoreType.DMA((4,)),
        ],
    )[0]


def space_grads(*args):
    return call(
        space_kernel,
        [(WIDTH, TOKENS)] * 3,
        args,
        4 * 10**10,
        60,
        grid=(4,),
        in_specs=[HEAD_PAIR] * 5,
        out_specs=(HEAD_PAIR,) * 3,
    )


def exchange(x, rows):
    x = x.reshape(FRAMES, rows, 128)
    x = lax.all_to_all(x, PEERS, split_axis=0, concat_axis=0, tiled=True)
    return x.reshape(FRAMES * rows, 128)


def body(*args):
    sq, sk, sv, so, sg, tq, tk, tv, to, tg = [jnp.swapaxes(x[0], 0, 1) for x in args]
    got = exchange(pack(tq, tk, tv, tg, to), SEND)
    space = space_grads(sq, sk, sv, so, sg)
    time = unpack(exchange(time_grads(got), BACK))
    return tuple(jnp.swapaxes(x, 0, 1)[None] for x in (*space, *time))


def solution(mesh):
    fine = Mesh(mesh.devices.reshape(-1, 8, 2, 4), ("dp", "z", "y", "x"))
    spec = P(("dp", "z", "y", "x"), None, None)
    return jax.shard_map(
        body, mesh=fine, in_specs=(spec,) * 10, out_specs=(spec,) * 6, check_vma=False
    )
```

```python
import math

import jax
import jax.numpy as jnp
from jax import lax
from jax.experimental import pallas as pl
from jax.experimental.pallas import tpu as pltpu
from jax.sharding import PartitionSpec as P

HEADS = 8
DIM = 72
WIDTH = HEADS * DIM
TOKENS = 704
FRAMES = 64
BULK = 512
EXTRA = TOKENS - BULK
SEND = 200
BACK = 152
UNITS = 22
ROWS = 4 * FRAMES
TILE = DIM // 8
SCALE = 1.0 / math.sqrt(DIM)
EXP_SCALE = SCALE * math.log2(math.e)
BF16 = jnp.bfloat16
F32 = jnp.float32
NN = ((1,), (0,))
NT = ((1,), (1,))
TN = ((0,), (0,))


def dot(a, b, dims):
    return lax.dot_general(a, b, (dims, ((), ())), preferred_element_type=F32)


def iota(shape, axis):
    return lax.broadcasted_iota(jnp.int32, shape, axis)


def ones_where(condition):
    return jnp.where(condition, 1.0, 0.0).astype(BF16)


def roll(x, shift):
    return pltpu.roll(x, shift, x.ndim - 1)


def turn(x, shift):
    return roll(x, shift % 128) if shift % 128 else x


def pack_kernel(q_ref, k_ref, v_ref, g_ref, o_ref, out_ref, held, made, picks, dot_pick, in_sem, out_sem):
    refs = (q_ref, k_ref, v_ref, g_ref, o_ref)

    def fetch(c, p):
        rows = pl.ds(pl.multiple_of(p * 2 * DIM, 16), 2 * DIM)
        return pltpu.make_async_copy(refs[c].at[rows, :], held.at[c, p], in_sem.at[c, p])

    def send(p):
        rows = pl.ds(pl.multiple_of(p * 2 * SEND, 16), 2 * SEND)
        return pltpu.make_async_copy(made.at[p], out_ref.at[:, rows, :], out_sem.at[p])

    for p in range(4):
        for c in range(5):
            fetch(c, p).start()

    row, lane = iota((EXTRA, 128), 0), iota((EXTRA, 128), 1)
    for a in range(8):
        at = row - 24 * a
        mine = (at >= 0) & (at < 24)
        cols = slice(128 * a, 128 * a + 128)
        dot_pick[:, cols] = ones_where(mine & (lane == 112 + at // 4))
        for i, c in enumerate((2, 3)):
            picks[i, :, cols] = ones_where(mine & (lane == at + 24 * c))
    token, lane = iota((128, 256), 0), iota((128, 256), 1)
    pick = (token // 64 == lane // 128) & ((token % 64) // 4 == lane % 128 - 96)
    pick = ones_where(pick)
    lane = iota((2 * DIM, 128), 1)
    body_lane = iota((2, 7, 8, 128), 3) < 96
    shape = (2, 8, TOKENS)
    same = iota(shape, 2) % 4 == iota(shape, 1) % 4

    def head_pair(p, carry):
        for c in range(5):
            fetch(c, p).wait()
        full = [held[c, p].astype(F32) for c in range(4)]
        dots = jnp.sum((full[3] * held[4, p].astype(F32)).reshape(2, DIM, TOKENS), axis=1)
        kept = jnp.where(same, dots[:, None, :], 0.0).reshape(16, TOKENS).astype(BF16)
        stacked = jnp.concatenate([kept[:, 128 * b : 128 * b + 128] for b in range(4)], axis=0)
        tail = dot(stacked, pick, NN)
        tail_more = dot(kept[:, BULK:], dot_pick[...], NN)
        spread = None
        for i, c in enumerate((2, 3)):
            part = dot(held[c, p, :, BULK:], picks[i], NN)
            spread = part if spread is None else spread + part
        fourth = [x[:, BULK : BULK + 128] for x in full]
        blank = jnp.zeros((2 * DIM, 64), F32)
        fifth = [jnp.concatenate([x[:, BULK + 128 :], blank], axis=1) for x in full]
        across = [jnp.where(lane < 16, x, y) for x, y in zip(fifth, fourth)]

        def gather(a):
            b, odd = a // 2, a % 2
            cols = slice(128 * b, 128 * b + 128)
            q, k, v, g = [x[:, cols] for x in full]
            pairs = []
            for x, y in ((q, k), (v, g)):
                if odd:
                    joined = jnp.where(lane < 64, roll(x, 64), y)
                else:
                    joined = jnp.where(lane < 64, x, roll(y, 64))
                pairs.append(joined.reshape(2, TILE, 8, 128))
            source = fourth if a < 5 else across if a == 5 else fifth
            rest = spread[:, 128 * a : 128 * a + 128]
            for c in range(4):
                if c not in (2, 3):
                    at = lane - 24 * c
                    rest = jnp.where((at >= 0) & (at < 24), turn(source[c], 24 * c - 24 * a), rest)
            return pairs, rest.reshape(2, TILE, 8, 128)

        def fold(a, pairs, rest):
            b, odd = a // 2, a % 2
            filler = [turn(rest[:, t], 96 - 32 * n) for t in (7, 8) for n in range(3)]
            here = tail[16 * b : 16 * b + 16, 128 * odd : 128 * odd + 128]
            here = here + tail_more[:, 128 * a : 128 * a + 128]
            filler.append(here.reshape(2, 8, 128))
            return pairs, rest[:, :7], jnp.stack(filler, axis=1)

        def store(a, pairs, rest, filler):
            rest = jnp.where(body_lane, rest, filler)
            message = jnp.concatenate([*pairs, rest], axis=1).reshape(2 * SEND, 128)
            made[p, a] = message.astype(BF16)

        first, second = {}, {}
        for t in range(10):
            if t % 2 == 0 and t < 8:
                first[t], first[t + 1] = gather(t), gather(t + 1)
            if 1 <= t < 9:
                second[t - 1] = fold(t - 1, *first.pop(t - 1))
            if t >= 2:
                store(t - 2, *second.pop(t - 2))
        send(p).start()
        return carry

    lax.fori_loop(0, 4, head_pair, 0)
    for p in range(4):
        send(p).wait()


def unpack_kernel(in_ref, dq_ref, dk_ref, dv_ref, made, sem):
    out_refs = (dq_ref, dk_ref, dv_ref)
    left = iota((2, TILE, 8, 128), 3) < 64
    lane = iota((2 * DIM, 128), 1)
    row = iota((64, 256), 0)
    end_pick = ones_where(iota((64, 256), 1) == 24 * (row // 8) + 16 + row % 8)

    def send(c, p):
        rows = pl.ds(pl.multiple_of(p * 2 * DIM, 16), 2 * DIM)
        return pltpu.make_async_copy(made.at[c, p], out_refs[c].at[rows, :], sem.at[c, p])

    def head_pair(p, carry):
        seconds, ends = [], []

        def gather(b):
            one, two = [
                in_ref[a, pl.ds(pl.multiple_of(p * 2 * BACK, 16), 2 * BACK), :].astype(F32).reshape(2, BACK // 8, 8, 128) for a in (2 * b, 2 * b + 1)
            ]
            first, second = one[:, :TILE], two[:, :TILE]
            third, fourth = one[:, TILE : 2 * TILE], two[:, TILE : 2 * TILE]
            seconds.extend([third.reshape(2 * DIM, 128), fourth.reshape(2 * DIM, 128)])
            ends.extend([one[:, 2 * TILE], two[:, 2 * TILE]])
            mixed = roll(jnp.where(left, second, first), 64)
            return (
                jnp.where(left, first, mixed),
                jnp.where(left, mixed, second),
                jnp.where(left, third, roll(fourth, 64)),
            )

        def store(b, grads):
            for c, grad in enumerate(grads):
                made[c, p, :, 128 * b : 128 * b + 128] = grad.reshape(2 * DIM, 128).astype(BF16)

        def shift(c):
            return [turn(x, 24 * a - 64 - 24 * c) for a, x in enumerate(seconds)]

        def join(c, moved):
            for tile, owners in ((0, range(6)), (1, range(5, 8))):
                total = last[:, 128 * tile : 128 * tile + 128]
                for a in owners:
                    at = lane - (24 * a - 128 * tile)
                    mine = (at >= 0) & (at < (24, 24, 16)[c])
                    total = jnp.where(mine, moved[a], total)
                start = BULK + 128 * tile
                part = total[:, : 128 - 64 * tile].astype(BF16)
                made[c, p, :, start : start + 128 - 64 * tile] = part

        ready = gather(0)
        for b in range(4):
            following = gather(b + 1) if b < 3 else None
            if b == 3:
                moved = shift(0)
            store(b, ready)
            ready = following
        ends = jnp.stack(ends, axis=1).reshape(2, 64, 128).astype(BF16)
        last = [dot(ends[h], end_pick, TN)[:DIM] for h in range(2)]
        last = jnp.concatenate(last, axis=0)
        for c in range(3):
            following = shift(c + 1) if c < 2 else None
            join(c, moved)
            send(c, p).start()
            moved = following
        return carry

    lax.fori_loop(0, 4, head_pair, 0, unroll=True)
    for p in range(4):
        for c in range(3):
            send(c, p).wait()


def softmax_t(scores):
    top = jnp.max(scores, axis=0, keepdims=True)
    weights = jnp.exp2((scores - top) * EXP_SCALE)
    return weights * (1.0 / jnp.sum(weights, axis=0, keepdims=True))


def time_kernel(in_ref, out_ref, held, tails, grads, made, out_sem):
    row = iota((256, 256), 0)
    order = ones_where(iota((256, 256), 1) == 128 * ((row // 4) % 2) + 4 * (row // 8) + row % 4)
    unit = ones_where(iota((DIM, DIM), 0) == iota((DIM, DIM), 1))
    lane = iota((8, 128), 1)
    upper = iota((8, 128), 0) < 4

    def arriving(j):
        firsts, rests, last = [], [], []
        for p in range(2):
            start = pl.multiple_of((2 * j + p) * 2 * SEND, 16)
            x = in_ref[pl.ds(start, 2 * SEND), :].astype(F32).reshape(2, SEND // 8, 8, 128)
            sides, more = [], []
            for f in range(2):
                sides.append(jnp.concatenate([x[f, :16], x[f, TILE:]], axis=0).reshape(256, 128))
                m = x[f, 2 * TILE :]
                ends = [
                    jnp.where(
                        lane < 32,
                        roll(m[t], 32),
                        jnp.where(lane < 64, roll(m[t + 1], 64), roll(m[t + 2], 96)),
                    )
                    for t in (0, 3)
                ]
                more.append(jnp.concatenate([m, ends[0][None], ends[1][None], m], axis=0))
            wide = jnp.concatenate(sides, axis=1).astype(BF16)
            firsts.append(wide)
            rests.append(jnp.concatenate([y.reshape(128, 128) for y in more], axis=1))
            last.append(jnp.where(upper, x[0, SEND // 8 - 1], x[1, SEND // 8 - 1]))
        rest = jnp.concatenate(rests, axis=0).astype(BF16)
        return firsts, rest, last

    def ordering(j, firsts, rest, last):
        return [dot(order, x, NT) for x in firsts], dot(order[: 8 * 4 * 6], rest, NT), last

    def keep(j, firsts, rest, last):
        at = pl.ds(pl.multiple_of(j * 16, 16), 16)
        for c in range(4):
            start = 128 * (c // 2)
            rows = slice(128 * (c % 2), 128 * (c % 2) + 128)
            halves = [x[rows, start : start + DIM].reshape(16, 8, DIM) for x in firsts]
            held[c, 0:16, at, 0:DIM] = jnp.concatenate(halves, axis=1).astype(BF16)
            rows = slice(48 * c, 48 * c + 48)
            halves = [rest[rows, x : x + DIM].reshape(6, 8, DIM) for x in (0, 128)]
            held[c, 16:UNITS, at, 0:DIM] = jnp.concatenate(halves, axis=1).astype(BF16)
        tails[at, :] = jnp.concatenate(last, axis=0)

    ahead(0, FRAMES // 4, 8, arriving, ordering, keep)
    pick = ones_where(iota((32, 128), 1) == iota((32, 128), 0) + 96)
    dots = dot(pick, tails[...].astype(BF16), NT)
    same = iota((ROWS, ROWS), 0) % 4 == iota((ROWS, ROWS), 1) % 4

    def load(u):
        q, k, v, g = [held[c, u, :, 0:DIM] for c in range(4)]
        return q, k, g, dot(k, q, NT), dot(v, g, NT)

    def middle(u, q, k, g, scores, grad_attend):
        attend = softmax_t(jnp.where(same, scores, -1e30))
        dscore = (attend * (grad_attend - dots[u : u + 1, :])).astype(BF16)
        return q, k, g, attend.astype(BF16), dscore

    def finish(u, q, k, g, attend, dscore):
        grads[0, u, :, 0:DIM] = dot(dscore, k, TN) * SCALE
        grads[1, u, :, 0:DIM] = dot(dscore, q, NN) * SCALE
        grads[2, u, :, 0:DIM] = dot(attend, g, NN)

    loaded, ready = load(0), None
    for u in range(UNITS + 1):
        following = load(u + 1) if u + 1 < UNITS else None
        if u > 0:
            finish(u - 1, *ready)
        if u < UNITS:
            ready = middle(u, *loaded)
        loaded = following

    def swap(x):
        pairs = x.reshape(x.shape[0] // 2, 2, 8, 128)
        even, odd = pairs[:, 0], pairs[:, 1]
        first = jnp.where(upper, even, pltpu.roll(odd, 4, 1))
        second = jnp.where(upper, pltpu.roll(even, 4, 1), odd)
        return first, second

    def leaving(i):
        at = pl.ds(pl.multiple_of(i * 8, 8), 8)
        sets = (
            (grads[0, 0:16, at, :], grads[1, 0:16, at, :]),
            (
                grads[2, 0:16, at, :],
                grads[0, 16:UNITS, at, :],
                grads[1, 16:UNITS, at, :],
                grads[2, 16:20, at, :],
            ),
        )
        turned = []
        for parts in sets:
            rows = jnp.concatenate(swap(jnp.concatenate(parts, axis=0)), axis=0)
            turned.append(rows.reshape(256, 128)[:, :DIM].astype(BF16))
        ends = swap(jnp.where(lane < DIM, grads[2, 20:22, at, :], 0.0))
        return turned, ends

    def turning(i, rows, ends):
        return [dot(unit, x, NT) for x in rows], ends

    def place(i, turned, ends):
        pieces = []
        for f in range(2):
            pieces += [t[:, 128 * f : 128 * f + 128] for t in turned] + [ends[f][0]]
        start = pl.multiple_of(i * 2 * BACK, 16)
        made[pl.ds(start, 2 * BACK), :] = jnp.concatenate(pieces, axis=0).astype(BF16)

    def send(part):
        rows = pl.ds(part * FRAMES * BACK // 4, FRAMES * BACK // 4)
        return pltpu.make_async_copy(made.at[rows, :], out_ref.at[rows, :], out_sem.at[part])

    for part in range(4):
        ahead(part, FRAMES // 8, 8, leaving, turning, place)
        send(part).start()
    for part in range(4):
        send(part).wait()


def ahead(part, count, block, make, work, use):
    def step(j, carry):
        base = part * count + j * block
        made, worked = {}, {}
        for t in range(block + 2):
            if t < block:
                made[t] = make(base + t)
            if 1 <= t <= block:
                worked[t - 1] = work(base + t - 1, *made.pop(t - 1))
            if t >= 2:
                use(base + t - 2, *worked.pop(t - 2))
        return carry

    lax.fori_loop(0, count // block, step, 0)


def space_kernel(q_ref, k_ref, v_ref, o_ref, g_ref, dq_ref, dk_ref, dv_ref):
    q2, k2, v2, o2, g2 = [ref[...].astype(F32) for ref in (q_ref, k_ref, v_ref, o_ref, g_ref)]
    dots = jnp.sum((g2 * o2).reshape(2, DIM, TOKENS), axis=1)
    grads = ([], [], [])
    for h in range(2):
        part = slice(h * DIM, (h + 1) * DIM)
        q, k, v, g = [x[part].astype(BF16) for x in (q2, k2, v2, g2)]
        k_rows, v_rows = k2[part].T.astype(BF16), v2[part].T.astype(BF16)
        dq, dk, dv = [], None, None
        for start, size in ((0, 256), (256, 256), (512, 192)):
            cols = slice(start, start + size)
            attend = softmax_t(dot(k_rows, q[:, cols], NN))
            shifted = dot(v_rows, g[:, cols], NN) - dots[h : h + 1, cols]
            dscore = (attend * shifted).astype(BF16)
            dq.append(dot(k, dscore, NN))
            dk_part = dot(q[:, cols], dscore, NT)
            dv_part = dot(g[:, cols], attend.astype(BF16), NT)
            dk = dk_part if dk is None else dk + dk_part
            dv = dv_part if dv is None else dv + dv_part
        grads[0].append(jnp.concatenate(dq, axis=1) * SCALE)
        grads[1].append(dk * SCALE)
        grads[2].append(dv)
    for ref, halves in zip((dq_ref, dk_ref, dv_ref), grads):
        ref[...] = jnp.concatenate(halves, axis=0).astype(BF16)


def call(kernel, out_shapes, args, flops, vmem, **specs):
    moved = sum(a.size * 2 for a in args) + sum(math.prod(o) * 2 for o in out_shapes)
    return pl.pallas_call(
        kernel,
        out_shape=tuple(jax.ShapeDtypeStruct(o, BF16) for o in out_shapes),
        compiler_params=pltpu.CompilerParams(vmem_limit_bytes=vmem * 1024 * 1024),
        cost_estimate=pl.CostEstimate(flops=flops, bytes_accessed=moved, transcendentals=0),
        name=kernel.__name__,
        **specs,
    )(*args)


HEAD_PAIR = pl.BlockSpec((2 * DIM, TOKENS), lambda p: (p, 0))


def pack(q, k, v, g, o):
    (sent,) = call(
        pack_kernel,
        [(8, HEADS * SEND, 128)],
        (q, k, v, g, o),
        10**9,
        60,
        in_specs=[pl.BlockSpec(memory_space=pltpu.HBM)] * 5,
        out_specs=(pl.BlockSpec(memory_space=pltpu.HBM),),
        scratch_shapes=[
            pltpu.VMEM((5, 4, 2 * DIM, TOKENS), BF16),
            pltpu.VMEM((4, 8, 2 * SEND, 128), BF16),
            pltpu.VMEM((2, EXTRA, 1024), BF16),
            pltpu.VMEM((EXTRA, 1024), BF16),
            pltpu.SemaphoreType.DMA((5, 4)),
            pltpu.SemaphoreType.DMA((4,)),
        ],
    )
    return sent


def unpack(back):
    return call(
        unpack_kernel,
        [(WIDTH, TOKENS)] * 3,
        (back.reshape(8, HEADS * BACK, 128),),
        10**9,
        50,
        in_specs=[pl.BlockSpec(memory_space=pltpu.VMEM)],
        out_specs=(pl.BlockSpec(memory_space=pltpu.HBM),) * 3,
        scratch_shapes=[
            pltpu.VMEM((3, 4, 2 * DIM, TOKENS), BF16),
            pltpu.SemaphoreType.DMA((3, 4)),
        ],
    )


def time_grads(got):
    return call(
        time_kernel,
        [(FRAMES * BACK, 128)],
        (got,),
        10**10,
        48,
        in_specs=[pl.BlockSpec(memory_space=pltpu.VMEM)],
        out_specs=(pl.BlockSpec(memory_space=pltpu.HBM),),
        scratch_shapes=[
            pltpu.VMEM((4, UNITS, ROWS, 128), BF16),
            pltpu.VMEM((ROWS, 128), F32),
            pltpu.VMEM((3, UNITS, ROWS, 128), F32),
            pltpu.VMEM((FRAMES * BACK, 128), BF16),
            pltpu.SemaphoreType.DMA((4,)),
        ],
    )[0]


def space_grads(half, args, before=()):
    spec = pl.BlockSpec((2 * DIM, TOKENS), lambda p: (2 * half + p, 0))

    def kernel(*refs):
        space_kernel(*refs[:5], *refs[-3:])

    kernel.__name__ = "space_kernel"
    return call(
        kernel,
        [(WIDTH, TOKENS)] * 3,
        (*args, *before),
        2 * 10**10,
        60,
        grid=(2,),
        in_specs=[spec] * 5 + [pl.BlockSpec(memory_space=pl.ANY)] * len(before),
        out_specs=(spec,) * 3,
        input_output_aliases={5 + n: n for n in range(len(before))},
    )


def exchange(x, rows):
    x = x.reshape(FRAMES, rows, 128)
    x = lax.all_to_all(x, "seq", split_axis=0, concat_axis=0, tiled=True)
    return x.reshape(FRAMES * rows, 128)


def body(*args):
    sq, sk, sv, so, sg, tq, tk, tv, to, tg = [jnp.swapaxes(x[0], 0, 1) for x in args]
    got = exchange(pack(tq, tk, tv, tg, to), SEND)
    early = space_grads(0, (sq, sk, sv, so, sg))
    got, early = lax.optimization_barrier((got, early))
    done, early = lax.optimization_barrier((time_grads(got), early))
    back = exchange(done, BACK)
    space = space_grads(1, (sq, sk, sv, so, sg), early)
    time = unpack(back)
    return tuple(jnp.swapaxes(x, 0, 1)[None] for x in (*space, *time))


def solution(mesh):
    spec = P(("dp", "seq"), None, None)
    return jax.shard_map(
        body, mesh=mesh, in_specs=(spec,) * 10, out_specs=(spec,) * 6, check_vma=False
    )
```
